128 devices in a mesh: peer: 2 (over core), dp: 4 (over y), tensor: 16 (over x, z).
Axes of the slice: x: 4, y: 4, z: 4, core: 2. Of those that a mesh axis runs over, the one named last changes fastest.
Arguments:
- hidden: bfloat16 [2, 512, 5120], P('peer', 'dp'), may hold values from -8 to 8
- gain: float32 [2, 5120], P('peer'), may hold values from 0.5 to 1.5
- head: bfloat16 [2, 5120, 81920], P('peer', None, ('dp', 'tensor'))
- targets: int32 [512], P('dp'), may hold values from 0 to 81919
- lengths: int32 [16], P('dp'), may hold values from 1 to 32
Outputs:
- loss: float32 [2], P('peer')
- grad_hidden: bfloat16 [2, 512, 5120], P('peer', 'dp')
The draws below stay inside these ranges and needn't reach their ends.
Inputs may be any that keep to these rules, and one draw needn't show every extreme that they name: `lengths`: the valid positions of a sequence are its first ones.
All inputs are finite; a program needn't handle non-finite values.
Results may differ from the reference program's by a relative error of at most 0.0071.
Values may be sent and summed in bfloat16 or wider, within the bound.
No kernel may reach another device: no remote copies, remote signals or barrier semaphores. Data moves between devices by JAX's collectives and lax.ppermute only.
A program may use at most 128 MiB of HBM per device.

```python
import math
import jax
import jax.numpy as jnp
import numpy as np
from jax import lax

D = 5120
LEN = 32
SEQS = 16
TOKENS = 512
VOCAB = 81920


def draw_hidden(key, part):
    key = jax.random.fold_in(key, 3)
    states = jnp.clip(jax.random.normal(key, (2, TOKENS, D), jnp.float32), -6.0, 6.0)
    return states.astype(jnp.bfloat16)


def draw_head(key, part):
    key = jax.random.fold_in(key, 5)
    spread = 3.0 / D ** 0.5
    matrix = jnp.clip(jax.random.normal(key, (2, D, VOCAB), jnp.float32), -6.0, 6.0) * spread
    return matrix.astype(jnp.bfloat16)


def with_ends(result, rng, smallest, high):
    longest = result.shape.index(max(result.shape))
    spots = []
    for shift in (0, 1):
        where = [jax.random.randint(jax.random.fold_in(rng, axis), (), 0, length) for axis, length in enumerate(result.shape)]
        where[longest] = (where[longest] + shift) % result.shape[longest]
        spots.append(tuple(where))
    return result.at[spots[0]].set(smallest).at[spots[1]].set(high)


def ranked_wide(rng, extent, number_of, skew):
    weights = [min(1 << octave, number_of + 1 - (1 << octave)) * (1 << 20) // math.isqrt((1 << octave) ** skew) + 1 for octave in range((number_of + 1).bit_length()) if 1 << octave <= number_of]
    width = 1 + sum(weights) // (1 << 30)
    table = np.cumsum(np.array([max(1, weight // width) for weight in weights]))
    ticket = jax.random.randint(jax.random.fold_in(rng, 1), extent, 0, int(table[len(weights) - 1]))
    start = jnp.left_shift(1, jnp.searchsorted(jnp.asarray(table, jnp.int32), ticket, side="right").astype(jnp.int32))
    grade = start - 1 + jax.random.randint(jax.random.fold_in(rng, 4), extent, 0, 1 << 30) % jnp.minimum(start, number_of + 1 - start)
    return jax.random.permutation(jax.random.fold_in(rng, 2), number_of)[grade].astype(jnp.int32)


def setup_inputs(seed: int = 0) -> dict:
    key_of = jax.random.split(jax.random.key(seed), 6)
    hidden = draw_hidden(jax.random.fold_in(key_of[5], 71), 0)
    gain = jnp.clip(1.0 + 0.1 * jax.random.normal(key_of[1], (2, D), jnp.float32), 0.5, 1.5)
    head = draw_head(jax.random.fold_in(key_of[5], 71), 0)
    targets = with_ends(ranked_wide(key_of[3], (TOKENS,), VOCAB, 2), jax.random.fold_in(key_of[3], 3), 0, VOCAB - 1).astype(jnp.int32)
    lengths = with_ends(jax.random.randint(key_of[4], (SEQS,), 1, LEN + 1), jax.random.fold_in(key_of[4], 1), 1, LEN).astype(jnp.int32)
    return dict(hidden=hidden, gain=gain, head=head, targets=targets, lengths=lengths)


kl_weight = 0.5
loss_scale = 64.0
eps_norm = 1e-06

def reference(hidden, gain, head, targets, lengths):
    states = hidden.astype(jnp.float32)
    inverse_rms = lax.rsqrt(lax.optimization_barrier(jnp.mean(states * states, axis=-1, keepdims=True)) + eps_norm)
    normed = (states * inverse_rms * gain[:, None, :]).astype(jnp.bfloat16)
    logits = jnp.stack([jnp.dot(normed[member], head[member], preferred_element_type=jnp.float32) for member in range(2)]).astype(jnp.bfloat16)
    values = logits.astype(jnp.float32)
    row_max = lax.optimization_barrier(jnp.max(values, axis=-1, keepdims=True))
    log_total = row_max + jnp.log(lax.optimization_barrier(jnp.sum(jnp.exp(values - row_max), axis=-1, keepdims=True)))
    probs = jnp.exp(values - log_total)
    peer_probs = probs[::-1]
    peer_values = values[::-1]
    peer_total = log_total[::-1]
    position = jnp.arange(TOKENS, dtype=jnp.int32)
    limits = lengths[position // LEN]
    weights = (position % LEN < limits).astype(jnp.float32)
    count = jnp.sum(weights)
    onehot = (jnp.arange(VOCAB, dtype=jnp.int32)[None, :] == targets[:, None]).astype(jnp.float32)
    target_logit = lax.optimization_barrier(jnp.sum(values * onehot[None], axis=-1))
    cross = lax.optimization_barrier(jnp.sum(peer_probs * (peer_values - values), axis=-1))
    per_token = log_total[..., 0] - target_logit + kl_weight * (cross - peer_total[..., 0] + log_total[..., 0])
    loss = lax.optimization_barrier(jnp.sum(per_token * weights[None], axis=-1)) / count
    grad_logits = (loss_scale * weights[None, :, None] * ((1.0 + kl_weight) * probs - onehot[None] - kl_weight * peer_probs)).astype(jnp.bfloat16)
    grad_normed = jnp.stack([lax.dot_general(grad_logits[member], head[member], (((1,), (1,)), ((), ())), preferred_element_type=jnp.float32) for member in range(2)])
    scaled = grad_normed * gain[:, None, :]
    inner = lax.optimization_barrier(jnp.mean(scaled * states, axis=-1, keepdims=True))
    grad_hidden = (inverse_rms * (scaled - states * inverse_rms * inverse_rms * inner)).astype(jnp.bfloat16)
    return (loss, grad_hidden)
```

```python
import jax
import jax.numpy as jnp
from jax import lax
from jax.experimental import pallas as pl
from jax.experimental.pallas import tpu as pltpu
from jax.sharding import Mesh, PartitionSpec as P

LEN = 32
TILE = 128

kl_weight = 0.5
loss_scale = 64.0
eps_norm = 1e-06

ALL = ("peer", "dp", "tx", "tz")

OWN, NEAR, WRAP, FAR = range(4)
FLIP = {1: 1, 2: 3, 3: 2}


def permute(block, move):
    def index(core, y, x, z):
        return ((core * 4 + y) * 4 + x) * 4 + z

    places = [(c, y, x, z) for c in range(2) for y in range(4) for x in range(4) for z in range(4)]
    return lax.ppermute(block, ALL, [(index(*p), index(*move(*p))) for p in places])


def swap_u(block, step):
    return permute(block, lambda c, y, x, z: (c, y, x ^ step, z) if c == 0 else (c, y, x, z ^ step))


def swap_y(block, steps):
    return permute(block, lambda c, y, x, z: (c, y ^ steps[c], x, z))


def core():
    return lax.axis_index("peer")


def by_core(first, second):
    return jnp.where(core() == 0, first, second)


def bits(position):
    return (position ^ (position >> 1)) & 1, position >> 1


def parity():
    return (lax.axis_index("tx") + lax.axis_index("tz")) & 1


def tied(*blocks):
    return lax.optimization_barrier(blocks)


def ring(block, axis):
    near, wrap, far = [lax.ppermute(block, axis, [(i, i ^ s) for i in range(4)]) for s in (1, 3, 2)]
    return [block, near, far, wrap]


def turned(block, step, axis):
    size = block.shape[axis] // 4
    parts = [lax.slice_in_dim(block, p * size, (p + 1) * size, axis=axis) for p in range(4)]
    return jnp.concatenate([parts[p ^ FLIP[step]] for p in range(4)], axis=axis)


def gather_logits(block, gain_row, matrix, ints):
    half = block.shape[0] // 2
    mine = lax.dynamic_slice_in_dim(block, parity() * half, half, axis=0)
    near = swap_y(mine, (1, 1))
    wrap = swap_y(mine, (3, 3))
    ints = ring(ints, "dp")
    logits = add_logits((block,), OWN_PLAN, gain_row, matrix, 3 * 128)
    near, wrap, logits, *ints = tied(near, wrap, logits, *ints)
    far = swap_y(by_core(wrap, near), (1, 3))
    pieces = [slice(k * half // 2, (k + 1) * half // 2) for k in range(2)]
    sides = [swap_u(jnp.concatenate([near[pieces[k]], wrap[pieces[k]]]), (1, 3)[k]) for k in range(2)]
    logits = add_logits((near, wrap), HELD_PLAN, gain_row, matrix, 3 * 128, logits)
    far, logits, *sides = tied(far, logits, *sides)
    far_sides = [swap_u(far[pieces[k]], (1, 3)[k]) for k in range(2)]
    logits = add_logits(sides, OTHER_PLAN, gain_row, matrix, 3 * 128, logits)
    logits, *far_sides = tied(logits, *far_sides)
    far_logits = add_logits((far, *far_sides), FAR_PLAN, gain_row, matrix, 128)
    return logits, far_logits, [ints[s] for s in (0, 1, 3, 2)]


CHUNKS = 10


def make_kernel(count, loads, stores):
    def kernel(*refs):
        sources = refs[:count]
        gain_ref, head_ref = refs[count : count + 2]
        out_ref, held_head, rows, sums, total, block, head_sems, sems = refs[-8:]
        width = rows.shape[1]
        deep = width // CHUNKS
        held = parity() * 64
        shift = {"all": 0, "held": held, "other": 64 - held}
        fetches = []
        for c in range(CHUNKS):
            piece = pl.ds(c * deep, deep)
            fetches.append(pltpu.make_async_copy(head_ref.at[piece], held_head.at[piece], head_sems.at[c]))
        copies = []
        for source, start, length, target, kind in loads:
            to = pl.multiple_of(shift[kind] + target, 16)
            copies.append(
                pltpu.make_async_copy(
                    sources[source].at[pl.ds(start, length)], rows.at[pl.ds(to, length)], sems.at[len(copies)]
                )
            )
        for copy in copies + fetches:
            copy.start()
        for copy in copies:
            copy.wait()

        @pl.loop(0, rows.shape[0] // 16)
        def _(step):
            piece = pl.ds(pl.multiple_of(step * 16, 16), 16)
            lanes = jnp.zeros((16, TILE), jnp.float32)
            for c in range(0, width, TILE):
                states = rows[piece, c : c + TILE].astype(jnp.float32)
                lanes += states * states
            sums[piece, :] = lanes

        mean = jnp.sum(sums[...], axis=-1, keepdims=True) / width
        sums[...] = jnp.broadcast_to(lax.rsqrt(mean + eps_norm), sums.shape)

        @pl.loop(0, rows.shape[0] // 16)
        def _(step):
            piece = pl.ds(pl.multiple_of(step * 16, 16), 16)
            inverse = sums[piece, :]
            for c in range(0, width, TILE):
                states = rows[piece, c : c + TILE].astype(jnp.float32)
                rows[piece, c : c + TILE] = (states * inverse * gain_ref[:, c : c + TILE]).astype(jnp.bfloat16)

        for c in range(0, CHUNKS, 2):
            fetches[c].wait()
            fetches[c + 1].wait()
            columns = slice(c * deep, (c + 2) * deep)
            part = jnp.dot(rows[:, columns], held_head[columns, :], preferred_element_type=jnp.float32)
            if c == 0:
                total[...] = part
            elif c < CHUNKS - 2:
                total[...] += part
            else:
                block[...] = (total[...] + part).astype(jnp.bfloat16)
        copies = []
        for start, length, target, kind in stores:
            to = pl.multiple_of(shift[kind] + target, 16)
            copies.append(
                pltpu.make_async_copy(
                    block.at[pl.ds(start, length)], out_ref.at[pl.ds(to, length)], sems.at[len(copies)]
                )
            )
        for copy in copies:
            copy.start()
        for copy in copies:
            copy.wait()

    return kernel


OWN_PLAN = [(0, 0, 128, 0, "all")], [(0, 128, 0, "all")]
HELD_PLAN = [(0, 0, 64, 0, "all"), (1, 0, 64, 64, "all")], [(0, 64, 128, "held"), (64, 64, 256, "held")]
OTHER_PLAN = (
    [(k, 32 * g, 32, 64 * g + 32 * k, "all") for k in range(2) for g in range(2)],
    [(0, 64, 128, "other"), (64, 64, 256, "other")],
)
FAR_PLAN = [(0, 0, 64, 0, "held")] + [(1 + k, 0, 32, 32 * k, "other") for k in range(2)], [(0, 128, 0, "all")]


def add_logits(sources, plan, gain_row, matrix, tokens, filled=None):
    width, voc = matrix.shape
    anywhere = pl.BlockSpec(memory_space=pl.ANY)
    count = len(sources)
    operands = [*sources, gain_row, matrix] + ([] if filled is None else [filled])
    return pl.pallas_call(
        make_kernel(count, *plan),
        out_shape=jax.ShapeDtypeStruct((tokens, voc), jnp.bfloat16),
        in_specs=[anywhere] * count
        + [pl.BlockSpec(memory_space=pltpu.VMEM), anywhere]
        + ([] if filled is None else [anywhere]),
        out_specs=anywhere,
        scratch_shapes=[
            pltpu.VMEM((width, voc), jnp.bfloat16),
            pltpu.VMEM((128, width), jnp.bfloat16),
            pltpu.VMEM((128, TILE), jnp.float32),
            pltpu.VMEM((128, voc), jnp.float32),
            pltpu.VMEM((128, voc), jnp.bfloat16),
            pltpu.SemaphoreType.DMA((CHUNKS,)),
            pltpu.SemaphoreType.DMA((4,)),
        ],
        input_output_aliases={} if filled is None else {count + 2: 0},
        compiler_params=pltpu.CompilerParams(vmem_limit_bytes=52 * 1024 * 1024),
        cost_estimate=pl.CostEstimate(
            flops=2 * 128 * width * voc, bytes_accessed=2 * width * (voc + 128), transcendentals=0
        ),
    )(*operands)


def merge(stats):
    stats = jnp.stack(stats)
    own_max = jnp.max(stats[:, 0], axis=0)
    peer_max = jnp.max(stats[:, 2], axis=0)
    own_scale = jnp.exp(stats[:, 0] - own_max)
    peer_scale = jnp.exp(stats[:, 2] - peer_max)
    (terms,) = tied(
        jnp.stack([stats[:, 1] * own_scale, stats[:, 3] * peer_scale, stats[:, 4], stats[:, 5] * peer_scale])
    )
    own_sum, peer_sum, target, cross = (terms[:, 0] + terms[:, 1]) + (terms[:, 2] + terms[:, 3])
    return jnp.stack([own_max, own_sum, peer_max, peer_sum, target, cross])


def wide(block):
    return block.astype(jnp.float32)


def narrow(block):
    return block.astype(jnp.bfloat16)


def sum_rows(grad_logits, matrix, later):
    voc = grad_logits.shape[1]
    width = matrix.shape[0] // 4
    at_x, at_z = bits(lax.axis_index("tx")), bits(lax.axis_index("tz"))
    rows = grad_logits.reshape(4, 4, 4, 8, voc)
    for axis in (1, 2):
        rows = jnp.concatenate([lax.slice_in_dim(rows, j, j + 1, axis=axis) for j in (0, 3, 1, 2)], axis=axis)
    rows = rows.reshape(4, 2, 2, 2, 2, 8, voc)
    dims = {"xa": (1, at_x[0], "tx", 1), "xb": (2, at_x[1], "tx", 3), "za": (3, at_z[0], "tz", 1), "zb": (4, at_z[1], "tz", 3)}
    orders = [("xa", "xb", "za", "zb"), ("xb", "xa", "zb", "za"), ("za", "zb", "xa", "xb"), ("zb", "za", "xb", "xa")]

    def product(block, q):
        columns = matrix[q * width : (q + 1) * width]
        out = lax.dot_general(
            block.reshape(-1, voc), columns, (((1,), (1,)), ((), ())), preferred_element_type=jnp.float32
        )
        return out.reshape(block.shape[:-1] + (width,))

    def split(block, name):
        at = dims[name][1]
        away = lax.dynamic_index_in_dim(block, 1 - at, 0, keepdims=False)
        return away, lax.dynamic_index_in_dim(block, at, 0, keepdims=False)

    def swap(block, name):
        axis, step = dims[name][2:]
        return lax.ppermute(block, axis, [(i, i ^ step) for i in range(4)])

    halves = []
    for order in orders:
        turned_rows = jnp.transpose(rows, [dims[name][0] for name in order] + [0, 5, 6])
        halves.append(split(turned_rows, order[0]))
    away = [narrow(product(*tied(halves[q][0]), q)) for q in range(4)]
    *stay, away[3] = tied(*[halves[q][1] for q in range(4)], away[3])
    came = [swap(away[q], orders[q][0]) for q in range(4)]
    kept = [product(stay[q], q) for q in range(4)]
    came[0], later = tied(came[0], later)
    for stage in range(1, 4):
        halves = [
            [k + wide(c) for k, c in zip(split(kept[q], orders[q][stage]), split(came[q], orders[q][stage]))]
            for q in range(4)
        ]
        came = [swap(narrow(halves[q][0]), orders[q][stage]) for q in range(4)]
        kept = [halves[q][1] for q in range(4)]
    state = [kept[q] + wide(came[q]) for q in range(4)]
    done = []
    for pair, first, second, steps in ((state[:2], NEAR, WRAP, (1, 3)), (state[2:], WRAP, NEAR, (3, 1))):
        block = jnp.concatenate(pair, axis=-1)
        came = swap_y(narrow(jnp.stack([block[first], block[FAR]])), (steps[0],) * 2)
        mine = block[OWN] + wide(came[0])
        came = swap_y(narrow(block[second] + wide(came[1])), (steps[1],) * 2)
        done.append(mine + wide(came))
    return jnp.concatenate(done, axis=-1), later


def shard_stats(logits, peer_logits, hit):
    values, peer_values = wide(logits), wide(peer_logits)
    own_max = jnp.max(values, axis=-1)
    peer_max = jnp.max(peer_values, axis=-1)
    peer_exp = jnp.exp(peer_values - peer_max[:, None])
    return jnp.stack(
        [
            own_max,
            jnp.sum(jnp.exp(values - own_max[:, None]), axis=-1),
            peer_max,
            jnp.sum(peer_exp, axis=-1),
            jnp.sum(jnp.where(hit, values, 0.0), axis=-1),
            jnp.sum(peer_exp * (peer_values - values), axis=-1),
        ]
    )


def mean_loss(stats, weights):
    own_log = stats[0] + jnp.log(stats[1])
    peer_log = stats[2] + jnp.log(stats[3])
    per_token = own_log - stats[4] + kl_weight * (stats[5] / stats[3] - peer_log + own_log)
    sums = jnp.sum((weights * per_token).reshape(4, -1), axis=-1)
    total = (sums[OWN] + sums[NEAR]) + (sums[FAR] + sums[WRAP])
    return (total / jnp.sum(weights)).reshape((1,))


def local(hidden, gain, head, targets, lengths):
    block = hidden[0]
    gain_row = gain[0][None, :]
    matrix = head[0]
    group = block.shape[0]
    tokens = 4 * group
    voc_shard = matrix.shape[1]
    first, second, ints = gather_logits(block, gain_row, matrix, jnp.concatenate([targets, lengths]))
    all_targets = jnp.concatenate([part[:group] for part in ints])
    all_lengths = jnp.concatenate([part[group:] for part in ints])
    hit = all_targets[:, None] - lax.axis_index(("dp", "tx", "tz")) * voc_shard
    hit = hit == lax.broadcasted_iota(jnp.int32, (1, voc_shard), 1)
    peer = [(0, 1), (1, 0)]
    first_peer, second_peer = lax.ppermute(first, "peer", peer), lax.ppermute(second, "peer", peer)
    cut = first.shape[0]
    stats = jnp.concatenate(
        [shard_stats(first, first_peer, hit[:cut]), shard_stats(second, second_peer, hit[cut:])], axis=1
    )
    stats = merge(ring(stats, "tz"))
    stats = merge(ring(stats, "tx"))
    stats = ring(stats, "dp")
    stats = merge([stats[0]] + [turned(stats[s], s, 1) for s in (1, 2, 3)])
    own_log = stats[0] + jnp.log(stats[1])
    peer_log = stats[2] + jnp.log(stats[3])
    values = wide(jnp.concatenate([first, second]))
    peer_values = wide(jnp.concatenate([first_peer, second_peer]))
    position = lax.broadcasted_iota(jnp.int32, (tokens // LEN, LEN), 1)
    weights = (position < all_lengths[:, None]).astype(jnp.float32).reshape(tokens)

    grad_logits = (
        loss_scale
        * weights[:, None]
        * (
            (1.0 + kl_weight) * jnp.exp(values - own_log[:, None])
            - hit.astype(jnp.float32)
            - kl_weight * jnp.exp(peer_values - peer_log[:, None])
        )
    ).astype(jnp.bfloat16)
    grad_normed, stats = sum_rows(grad_logits, matrix, stats)
    loss = mean_loss(stats, weights)

    own = wide(lax.dynamic_slice_in_dim(block, lax.axis_index(("tx", "tz")) * 8, 8, axis=0))
    own_inverse = lax.rsqrt(jnp.mean(own * own, axis=-1, keepdims=True) + eps_norm)
    scaled = grad_normed * gain_row
    inner = jnp.mean(scaled * own, axis=-1, keepdims=True)
    rows = narrow(own_inverse * (scaled - own * own_inverse * own_inverse * inner))
    spread = jnp.broadcast_to(rows[None], (16,) + rows.shape)
    grad_hidden = lax.all_to_all(spread, ("tx", "tz"), split_axis=0, concat_axis=0, tiled=True)
    return (loss, grad_hidden.reshape((1,) + block.shape))


def solution(mesh):
    cube = Mesh(mesh.devices.reshape(2, 4, 4, 4), ALL)
    return jax.shard_map(
        local,
        mesh=cube,
        in_specs=(
            P("peer", "dp", None),
            P("peer", None),
            P("peer", None, ("dp", "tx", "tz")),
            P("dp"),
            P("dp"),
        ),
        out_specs=(P("peer"), P("peer", "dp", None)),
        check_vma=False,
    )
```

```python
import functools

import jax
import jax.numpy as jnp
from jax import lax
from jax.experimental import pallas as pl
from jax.experimental.pallas import tpu as pltpu
from jax.sharding import Mesh, PartitionSpec as P

LEN = 32
TILE = 128

kl_weight = 0.5
loss_scale = 64.0
eps_norm = 1e-06

ALL = ("peer", "dp", "tx", "tz")

OWN, NEAR, WRAP, FAR = range(4)
FLIP = {1: 1, 2: 3, 3: 2}


def permute(block, move):
    def index(core, y, x, z):
        return ((core * 4 + y) * 4 + x) * 4 + z

    places = [(c, y, x, z) for c in range(2) for y in range(4) for x in range(4) for z in range(4)]
    return lax.ppermute(block, ALL, [(index(*p), index(*move(*p))) for p in places])


def swap_u(block, step):
    return permute(block, lambda c, y, x, z: (c, y, x ^ step, z) if c == 0 else (c, y, x, z ^ step))


def swap_y(block, steps):
    return permute(block, lambda c, y, x, z: (c, y ^ steps[c], x, z))


def core():
    return lax.axis_index("peer")


def by_core(first, second):
    return jnp.where(core() == 0, first, second)


def bits(position):
    return (position ^ (position >> 1)) & 1, position >> 1


def parity():
    return (lax.axis_index("tx") + lax.axis_index("tz")) & 1


def tied(*blocks):
    return lax.optimization_barrier(blocks)


def ring(block, axis):
    near, wrap, far = [lax.ppermute(block, axis, [(i, i ^ s) for i in range(4)]) for s in (1, 3, 2)]
    return [block, near, far, wrap]


def turned(block, step, axis):
    size = block.shape[axis] // 4
    parts = [lax.slice_in_dim(block, p * size, (p + 1) * size, axis=axis) for p in range(4)]
    return jnp.concatenate([parts[p ^ FLIP[step]] for p in range(4)], axis=axis)


def gather_logits(block, gain_row, matrix, ints):
    half = block.shape[0] // 2
    tokens = 4 * block.shape[0]
    mine = lax.dynamic_slice_in_dim(block, parity() * half, half, axis=0)
    p = swap_y(mine, (1, 3))
    q = swap_y(mine, (3, 1))
    ints = ring(ints, "dp")
    logits = add_logits((block,), OWN_PLAN, gain_row, matrix, tokens)
    p, q, logits, *ints = tied(p, q, logits, *ints)
    far = swap_y(q, (1, 3))
    p_side, q_side = swap_u(p, 1), swap_u(q, 3)
    logits = add_logits((p, q), HELD_PLAN, gain_row, matrix, tokens, logits)
    far, logits, p_side, q_side = tied(far, logits, p_side, q_side)
    far_sides = [swap_u(far[: half // 2], 1), swap_u(far[half // 2 :], 3)]
    logits = add_logits((p_side, q_side), OTHER_PLAN, gain_row, matrix, tokens, logits)
    logits = add_logits((far, *far_sides), FAR_PLAN, gain_row, matrix, tokens, logits)
    return logits, [ints[s] for s in (0, 1, 3, 2)]


CHUNKS = 10


def make_kernel(count, loads, stores):
    def kernel(*refs):
        sources = refs[:count]
        gain_ref, head_ref = refs[count : count + 2]
        out_ref, held_head, rows, sums, total, block, head_sems, sems = refs[-8:]
        width = rows.shape[1]
        deep = width // CHUNKS
        held = parity() * 64
        p_first = 128 * (NEAR + core() * (WRAP - NEAR))
        q_first = 128 * (NEAR + WRAP) - p_first
        shift = {"all": 0, "held": held, "other": 64 - held}
        shift |= {"p held": p_first + held, "q held": q_first + held}
        shift |= {"p other": p_first + 64 - held, "q other": q_first + 64 - held}
        fetches = []
        for c in range(CHUNKS):
            piece = pl.ds(c * deep, deep)
            fetches.append(pltpu.make_async_copy(head_ref.at[piece], held_head.at[piece], head_sems.at[c]))
        copies = []
        for source, start, length, target, kind in loads:
            to = pl.multiple_of(shift[kind] + target, 16)
            copies.append(
                pltpu.make_async_copy(
                    sources[source].at[pl.ds(start, length)], rows.at[pl.ds(to, length)], sems.at[len(copies)]
                )
            )
        for copy in copies + fetches:
            copy.start()
        for copy in copies:
            copy.wait()

        @pl.loop(0, rows.shape[0] // 16)
        def _(step):
            piece = pl.ds(pl.multiple_of(step * 16, 16), 16)
            lanes = jnp.zeros((16, TILE), jnp.float32)
            for c in range(0, width, TILE):
                states = rows[piece, c : c + TILE].astype(jnp.float32)
                lanes += states * states
            sums[piece, :] = lanes

        mean = jnp.sum(sums[...], axis=-1, keepdims=True) / width
        sums[...] = jnp.broadcast_to(lax.rsqrt(mean + eps_norm), sums.shape)

        @pl.loop(0, rows.shape[0] // 16)
        def _(step):
            piece = pl.ds(pl.multiple_of(step * 16, 16), 16)
            inverse = sums[piece, :]
            for c in range(0, width, TILE):
                states = rows[piece, c : c + TILE].astype(jnp.float32)
                rows[piece, c : c + TILE] = (states * inverse * gain_ref[:, c : c + TILE]).astype(jnp.bfloat16)

        for c in range(0, CHUNKS, 2):
            fetches[c].wait()
            fetches[c + 1].wait()
            columns = slice(c * deep, (c + 2) * deep)
            part = jnp.dot(rows[:, columns], held_head[columns, :], preferred_element_type=jnp.float32)
            if c == 0:
                total[...] = part
            elif c < CHUNKS - 2:
                total[...] += part
            else:
                block[...] = (total[...] + part).astype(jnp.bfloat16)
        copies = []
        for start, length, target, kind in stores:
            to = pl.multiple_of(shift[kind] + target, 16)
            copies.append(
                pltpu.make_async_copy(
                    block.at[pl.ds(start, length)], out_ref.at[pl.ds(to, length)], sems.at[len(copies)]
                )
            )
        for copy in copies:
            copy.start()
        for copy in copies:
            copy.wait()

    return kernel


OWN_PLAN = [(0, 0, 128, 0, "all")], [(0, 128, 0, "all")]
HELD_PLAN = [(0, 0, 64, 0, "all"), (1, 0, 64, 64, "all")], [(0, 64, 0, "p held"), (64, 64, 0, "q held")]
OTHER_PLAN = [(0, 0, 64, 0, "all"), (1, 0, 64, 64, "all")], [(0, 64, 0, "p other"), (64, 64, 0, "q other")]
FAR_PLAN = (
    [(0, 0, 64, 0, "held")] + [(1 + k, 0, 32, 32 * k, "other") for k in range(2)],
    [(0, 128, FAR * 128, "all")],
)


def add_logits(sources, plan, gain_row, matrix, tokens, filled=None):
    width, voc = matrix.shape
    anywhere = pl.BlockSpec(memory_space=pl.ANY)
    count = len(sources)
    rows = sum(piece[2] for piece in plan[0])
    operands = [*sources, gain_row, matrix] + ([] if filled is None else [filled])
    return pl.pallas_call(
        make_kernel(count, *plan),
        out_shape=jax.ShapeDtypeStruct((tokens, voc), jnp.bfloat16),
        in_specs=[anywhere] * count
        + [pl.BlockSpec(memory_space=pltpu.VMEM), anywhere]
        + ([] if filled is None else [anywhere]),
        out_specs=anywhere,
        scratch_shapes=[
            pltpu.VMEM((width, voc), jnp.bfloat16),
            pltpu.VMEM((rows, width), jnp.bfloat16),
            pltpu.VMEM((rows, TILE), jnp.float32),
            pltpu.VMEM((rows, voc), jnp.float32),
            pltpu.VMEM((rows, voc), jnp.bfloat16),
            pltpu.SemaphoreType.DMA((CHUNKS,)),
            pltpu.SemaphoreType.DMA((5,)),
        ],
        input_output_aliases={} if filled is None else {count + 2: 0},
        compiler_params=pltpu.CompilerParams(vmem_limit_bytes=52 * 1024 * 1024),
        cost_estimate=pl.CostEstimate(
            flops=2 * rows * width * voc, bytes_accessed=2 * width * (voc + rows), transcendentals=0
        ),
    )(*operands)


def merge(stats):
    stats = jnp.stack(stats)
    own_max = jnp.max(stats[:, 0], axis=0)
    peer_max = jnp.max(stats[:, 2], axis=0)
    own_scale = jnp.exp(stats[:, 0] - own_max)
    peer_scale = jnp.exp(stats[:, 2] - peer_max)
    (terms,) = tied(
        jnp.stack([stats[:, 1] * own_scale, stats[:, 3] * peer_scale, stats[:, 4], stats[:, 5] * peer_scale])
    )
    own_sum, peer_sum, target, cross = (terms[:, 0] + terms[:, 1]) + (terms[:, 2] + terms[:, 3])
    return jnp.stack([own_max, own_sum, peer_max, peer_sum, target, cross])


def wide(block):
    return block.astype(jnp.float32)


def narrow(block):
    return block.astype(jnp.bfloat16)


def away_kernel(*refs):
    sources, head_ref, outs = refs[:4], refs[4], refs[5:9]
    held_head, blocks, results, head_sems, in_sems, out_sems = refs[9:]
    deep = head_ref.shape[0] // 8
    fetches, loads, stores = [], [], []
    for q in range(4):
        loads.append(pltpu.make_async_copy(sources[q], blocks.at[q], in_sems.at[q]))
        for c in (2 * q, 2 * q + 1):
            piece = pl.ds(c * deep, deep)
            fetches.append(pltpu.make_async_copy(head_ref.at[piece], held_head.at[piece], head_sems.at[c]))
    for copy in loads[:1] + fetches[:2] + loads[1:] + fetches[2:]:
        copy.start()
    for q in range(4):
        loads[q].wait()
        for c in (2 * q, 2 * q + 1):
            fetches[c].wait()
        columns = held_head[2 * q * deep : 2 * (q + 1) * deep, :]
        out = lax.dot_general(blocks[q], columns, (((1,), (1,)), ((), ())), preferred_element_type=jnp.float32)
        results[q] = narrow(out)
        stores.append(pltpu.make_async_copy(results.at[q], outs[q], out_sems.at[q]))
        stores[q].start()
    for copy in stores:
        copy.wait()


def away_products(blocks, matrix):
    width, voc = matrix.shape
    rows, columns = blocks[0].shape[0], width // 4
    anywhere = pl.BlockSpec(memory_space=pl.ANY)
    return pl.pallas_call(
        away_kernel,
        out_shape=[jax.ShapeDtypeStruct((rows, columns), jnp.bfloat16)] * 4,
        in_specs=[anywhere] * 5,
        out_specs=[anywhere] * 4,
        scratch_shapes=[
            pltpu.VMEM((width, voc), jnp.bfloat16),
            pltpu.VMEM((4, rows, voc), jnp.bfloat16),
            pltpu.VMEM((4, rows, columns), jnp.bfloat16),
            pltpu.SemaphoreType.DMA((8,)),
            pltpu.SemaphoreType.DMA((4,)),
            pltpu.SemaphoreType.DMA((4,)),
        ],
        compiler_params=pltpu.CompilerParams(vmem_limit_bytes=52 * 1024 * 1024),
        cost_estimate=pl.CostEstimate(
            flops=2 * rows * width * voc, bytes_accessed=2 * (width * voc + rows * (width + 4 * voc)), transcendentals=0
        ),
    )(*blocks, matrix)


def sum_rows(grad_logits, matrix, later):
    voc = grad_logits.shape[1]
    width = matrix.shape[0] // 4
    at_x, at_z = bits(lax.axis_index("tx")), bits(lax.axis_index("tz"))
    rows = grad_logits.reshape(4, 4, 4, 8, voc)
    for axis in (1, 2):
        rows = jnp.concatenate([lax.slice_in_dim(rows, j, j + 1, axis=axis) for j in (0, 3, 1, 2)], axis=axis)
    rows = rows.reshape(4, 2, 2, 2, 2, 8, voc)
    dims = {"xa": (1, at_x[0], "tx", 1), "xb": (2, at_x[1], "tx", 3), "za": (3, at_z[0], "tz", 1), "zb": (4, at_z[1], "tz", 3)}
    orders = [("xa", "xb", "za", "zb"), ("xb", "xa", "zb", "za"), ("za", "zb", "xa", "xb"), ("zb", "za", "xb", "xa")]

    def product(block, q):
        columns = matrix[q * width : (q + 1) * width]
        out = lax.dot_general(
            block.reshape(-1, voc), columns, (((1,), (1,)), ((), ())), preferred_element_type=jnp.float32
        )
        return out.reshape(block.shape[:-1] + (width,))

    def split(block, name):
        at = dims[name][1]
        away = lax.dynamic_index_in_dim(block, 1 - at, 0, keepdims=False)
        return away, lax.dynamic_index_in_dim(block, at, 0, keepdims=False)

    def swap(block, name):
        axis, step = dims[name][2:]
        return lax.ppermute(block, axis, [(i, i ^ step) for i in range(4)])

    away, stay = [], []
    for order in orders:
        turned_rows = jnp.transpose(rows, [dims[name][0] for name in order] + [0, 5, 6])
        one, other = split(turned_rows, order[0])
        away.append(one.reshape(-1, voc))
        stay.append(other)
    shape = stay[0].shape[:-1] + (width,)
    came = [swap(block.reshape(shape), order[0]) for block, order in zip(away_products(away, matrix), orders)]
    kept = [product(stay[q], q) for q in range(4)]
    came[0], later = tied(came[0], later)
    for stage in range(1, 4):
        halves = [
            [k + wide(c) for k, c in zip(split(kept[q], orders[q][stage]), split(came[q], orders[q][stage]))]
            for q in range(4)
        ]
        came = [swap(narrow(halves[q][0]), orders[q][stage]) for q in range(4)]
        kept = [halves[q][1] for q in range(4)]
    state = [kept[q] + wide(came[q]) for q in range(4)]
    done = []
    for pair, first, second, steps in ((state[:2], NEAR, WRAP, (1, 3)), (state[2:], WRAP, NEAR, (3, 1))):
        block = jnp.concatenate(pair, axis=-1)
        came = swap_y(narrow(jnp.stack([block[first], block[FAR]])), (steps[0],) * 2)
        mine = block[OWN] + wide(came[0])
        came = swap_y(narrow(block[second] + wide(came[1])), (steps[1],) * 2)
        done.append(mine + wide(came))
    return done, later


def shard_stats(logits, peer_logits, hit):
    values, peer_values = wide(logits), wide(peer_logits)
    own_max = jnp.max(values, axis=-1)
    peer_max = jnp.max(peer_values, axis=-1)
    peer_exp = jnp.exp(peer_values - peer_max[:, None])
    return jnp.stack(
        [
            own_max,
            jnp.sum(jnp.exp(values - own_max[:, None]), axis=-1),
            peer_max,
            jnp.sum(peer_exp, axis=-1),
            jnp.sum(jnp.where(hit, values, 0.0), axis=-1),
            jnp.sum(peer_exp * (peer_values - values), axis=-1),
        ]
    )


def norm_backward_kernel(count, *refs):
    states_ref, gain_ref, out_ref = refs[count:]
    states = states_ref[...]
    width = states.shape[1]
    inverse = lax.rsqrt(jnp.sum(states * states, axis=-1, keepdims=True) / width + eps_norm)
    pieces, start = [], 0
    for ref in refs[:count]:
        columns = slice(start, start + ref.shape[1])
        pieces.append((ref[...] * gain_ref[:, columns], columns))
        start += ref.shape[1]
    inner = sum(jnp.sum(scaled * states[:, columns], axis=-1, keepdims=True) for scaled, columns in pieces) / width
    for scaled, columns in pieces:
        rows = narrow(inverse * (scaled - states[:, columns] * inverse * inverse * inner))
        for k in range(out_ref.shape[0]):
            out_ref[k, :, columns] = rows


def mean_loss(stats, weights):
    own_log = stats[0] + jnp.log(stats[1])
    peer_log = stats[2] + jnp.log(stats[3])
    per_token = own_log - stats[4] + kl_weight * (stats[5] / stats[3] - peer_log + own_log)
    sums = jnp.sum((weights * per_token).reshape(4, -1), axis=-1)
    total = (sums[OWN] + sums[NEAR]) + (sums[FAR] + sums[WRAP])
    return (total / jnp.sum(weights)).reshape((1,))


def local(hidden, gain, head, targets, lengths):
    block = hidden[0]
    gain_row = gain[0][None, :]
    matrix = head[0]
    group = block.shape[0]
    tokens = 4 * group
    voc_shard = matrix.shape[1]
    logits, ints = gather_logits(block, gain_row, matrix, jnp.concatenate([targets, lengths]))
    all_targets = jnp.concatenate([part[:group] for part in ints])
    all_lengths = jnp.concatenate([part[group:] for part in ints])
    peer_logits = lax.ppermute(logits, "peer", [(0, 1), (1, 0)])
    hit = all_targets[:, None] - lax.axis_index(("dp", "tx", "tz")) * voc_shard
    hit = hit == lax.broadcasted_iota(jnp.int32, (1, voc_shard), 1)
    stats = shard_stats(logits, peer_logits, hit)
    stats = merge(ring(stats, "tz"))
    stats = merge(ring(stats, "tx"))
    stats = ring(stats, "dp")
    stats = merge([stats[0]] + [turned(stats[s], s, 1) for s in (1, 2, 3)])
    own_log = stats[0] + jnp.log(stats[1])
    peer_log = stats[2] + jnp.log(stats[3])
    values, peer_values = wide(logits), wide(peer_logits)
    position = lax.broadcasted_iota(jnp.int32, (tokens // LEN, LEN), 1)
    weights = (position < all_lengths[:, None]).astype(jnp.float32).reshape(tokens)

    grad_logits = (
        loss_scale
        * weights[:, None]
        * (
            (1.0 + kl_weight) * jnp.exp(values - own_log[:, None])
            - hit.astype(jnp.float32)
            - kl_weight * jnp.exp(peer_values - peer_log[:, None])
        )
    ).astype(jnp.bfloat16)
    grad_normed, stats = sum_rows(grad_logits, matrix, stats)
    loss = mean_loss(stats, weights)

    own = lax.dynamic_slice_in_dim(block, lax.axis_index(("tx", "tz")) * 8, 8, axis=0)
    spread = pl.pallas_call(
        functools.partial(norm_backward_kernel, len(grad_normed)),
        out_shape=jax.ShapeDtypeStruct((16,) + own.shape, own.dtype),
        compiler_params=pltpu.CompilerParams(vmem_limit_bytes=16 * 1024 * 1024),
    )(*grad_normed, wide(own), gain_row)
    grad_hidden = lax.all_to_all(spread, ("tx", "tz"), split_axis=0, concat_axis=0, tiled=True)
    return (loss, grad_hidden.reshape((1,) + block.shape))


def solution(mesh):
    cube = Mesh(mesh.devices.reshape(2, 4, 4, 4), ALL)
    return jax.shard_map(
        local,
        mesh=cube,
        in_specs=(
            P("peer", "dp", None),
            P("peer", None),
            P("peer", None, ("dp", "tx", "tz")),
            P("dp"),
            P("dp"),
        ),
        out_specs=(P("peer"), P("peer", "dp", None)),
        check_vma=False,
    )
```

```python
import functools

import jax
import jax.numpy as jnp
from jax import lax
from jax.experimental import pallas as pl
from jax.experimental.pallas import tpu as pltpu
from jax.sharding import Mesh, PartitionSpec as P

LEN = 32
TILE = 128

kl_weight = 0.5
loss_scale = 64.0
eps_norm = 1e-06

ALL = ("peer", "dp", "tx", "tz")

OWN, NEAR, WRAP, FAR = range(4)
FLIP = {1: 1, 2: 3, 3: 2}


def permute(block, move):
    def index(core, y, x, z):
        return ((core * 4 + y) * 4 + x) * 4 + z

    places = [(c, y, x, z) for c in range(2) for y in range(4) for x in range(4) for z in range(4)]
    return lax.ppermute(block, ALL, [(index(*p), index(*move(*p))) for p in places])


def swap_u(block, step):
    return permute(block, lambda c, y, x, z: (c, y, x ^ step, z) if c == 0 else (c, y, x, z ^ step))


def swap_y(block, steps):
    return permute(block, lambda c, y, x, z: (c, y ^ steps[c], x, z))


def core():
    return lax.axis_index("peer")


def by_core(first, second):
    return jnp.where(core() == 0, first, second)


def bits(position):
    return (position ^ (position >> 1)) & 1, position >> 1


def parity():
    return (lax.axis_index("tx") + lax.axis_index("tz")) & 1


def tied(*blocks):
    return lax.optimization_barrier(blocks)


def ring(block, axis):
    near, wrap, far = [lax.ppermute(block, axis, [(i, i ^ s) for i in range(4)]) for s in (1, 3, 2)]
    return [block, near, far, wrap]


def turned(block, step, axis):
    size = block.shape[axis] // 4
    parts = [lax.slice_in_dim(block, p * size, (p + 1) * size, axis=axis) for p in range(4)]
    return jnp.concatenate([parts[p ^ FLIP[step]] for p in range(4)], axis=axis)


def gather_logits(block, gain_row, matrix, ints):
    half = block.shape[0] // 2
    tokens = 4 * block.shape[0]
    mine = lax.dynamic_slice_in_dim(block, parity() * half, half, axis=0)
    p = swap_y(mine, (1, 3))
    q = swap_y(mine, (3, 1))
    ints = ring(ints, "dp")
    logits = add_logits((block,), OWN_PLAN, gain_row, matrix, tokens)
    p, q, logits, *ints = tied(p, q, logits, *ints)
    far = swap_y(q, (1, 3))
    p_side, q_side = swap_u(p, 1), swap_u(q, 3)
    logits = add_logits((p, q), HELD_PLAN, gain_row, matrix, tokens, logits)
    far, logits, p_side, q_side = tied(far, logits, p_side, q_side)
    far_sides = [swap_u(far[: half // 2], 1), swap_u(far[half // 2 :], 3)]
    logits = add_logits((p_side, q_side), OTHER_PLAN, gain_row, matrix, tokens, logits)
    logits = add_logits((far, *far_sides), FAR_PLAN, gain_row, matrix, tokens, logits)
    return logits, [ints[s] for s in (0, 1, 3, 2)]


CHUNKS = 10


def make_kernel(count, streamed, loads, stores):
    def kernel(*refs):
        sources = refs[:count]
        gain_ref, head_ref = refs[count : count + 2]
        out_ref, rows, sums, total, block, sems = refs[len(refs) - 6 :] if not streamed else refs[-8:-2]
        held_head, head_sems = refs[-2:] if streamed else (head_ref, None)
        width = rows.shape[1]
        deep = width // CHUNKS
        held = parity() * 64
        p_first = 128 * (NEAR + core() * (WRAP - NEAR))
        q_first = 128 * (NEAR + WRAP) - p_first
        shift = {"all": 0, "held": held, "other": 64 - held}
        shift |= {"p held": p_first + held, "q held": q_first + held}
        shift |= {"p other": p_first + 64 - held, "q other": q_first + 64 - held}
        fetches = []
        for c in range(CHUNKS if streamed else 0):
            piece = pl.ds(c * deep, deep)
            fetches.append(pltpu.make_async_copy(head_ref.at[piece], held_head.at[piece], head_sems.at[c]))
        copies = []
        for source, start, length, target, kind in loads:
            to = pl.multiple_of(shift[kind] + target, 16)
            copies.append(
                pltpu.make_async_copy(
                    sources[source].at[pl.ds(start, length)], rows.at[pl.ds(to, length)], sems.at[len(copies)]
                )
            )
        for copy in copies + fetches:
            copy.start()
        for copy in copies:
            copy.wait()

        @pl.loop(0, rows.shape[0] // 16)
        def _(step):
            piece = pl.ds(pl.multiple_of(step * 16, 16), 16)
            lanes = jnp.zeros((16, TILE), jnp.float32)
            for c in range(0, width, TILE):
                states = rows[piece, c : c + TILE].astype(jnp.float32)
                lanes += states * states
            sums[piece, :] = lanes

        mean = jnp.sum(sums[...], axis=-1, keepdims=True) / width
        sums[...] = jnp.broadcast_to(lax.rsqrt(mean + eps_norm), sums.shape)

        @pl.loop(0, rows.shape[0] // 16)
        def _(step):
            piece = pl.ds(pl.multiple_of(step * 16, 16), 16)
            inverse = sums[piece, :]
            for c in range(0, width, TILE):
                states = rows[piece, c : c + TILE].astype(jnp.float32)
                rows[piece, c : c + TILE] = (states * inverse * gain_ref[:, c : c + TILE]).astype(jnp.bfloat16)

        for c in range(0, CHUNKS, 2):
            for copy in fetches[c : c + 2]:
                copy.wait()
            columns = slice(c * deep, (c + 2) * deep)
            part = jnp.dot(rows[:, columns], held_head[columns, :], preferred_element_type=jnp.float32)
            if c == 0:
                total[...] = part
            elif c < CHUNKS - 2:
                total[...] += part
            else:
                block[...] = (total[...] + part).astype(jnp.bfloat16)
        copies = []
        for start, length, target, kind in stores:
            to = pl.multiple_of(shift[kind] + target, 16)
            copies.append(
                pltpu.make_async_copy(
                    block.at[pl.ds(start, length)], out_ref.at[pl.ds(to, length)], sems.at[len(copies)]
                )
            )
        for copy in copies:
            copy.start()
        for copy in copies:
            copy.wait()

    return kernel


OWN_PLAN = [(0, 0, 128, 0, "all")], [(0, 128, 0, "all")]
HELD_PLAN = [(0, 0, 64, 0, "all"), (1, 0, 64, 64, "all")], [(0, 64, 0, "p held"), (64, 64, 0, "q held")]
OTHER_PLAN = [(0, 0, 64, 0, "all"), (1, 0, 64, 64, "all")], [(0, 64, 0, "p other"), (64, 64, 0, "q other")]
FAR_PLAN = (
    [(0, 0, 64, 0, "held")] + [(1 + k, 0, 32, 32 * k, "other") for k in range(2)],
    [(0, 128, FAR * 128, "all")],
)


def add_logits(sources, plan, gain_row, matrix, tokens, filled=None):
    width, voc = matrix.shape
    anywhere = pl.BlockSpec(memory_space=pl.ANY)
    count = len(sources)
    rows = sum(piece[2] for piece in plan[0])
    streamed = filled is None
    operands = [*sources, gain_row, matrix] + ([] if filled is None else [filled])
    return pl.pallas_call(
        make_kernel(count, streamed, *plan),
        out_shape=jax.ShapeDtypeStruct((tokens, voc), jnp.bfloat16),
        in_specs=[anywhere] * count
        + [pl.BlockSpec(memory_space=pltpu.VMEM), anywhere if streamed else pl.BlockSpec(memory_space=pltpu.VMEM)]
        + ([] if filled is None else [anywhere]),
        out_specs=anywhere,
        scratch_shapes=[
            pltpu.VMEM((rows, width), jnp.bfloat16),
            pltpu.VMEM((rows, TILE), jnp.float32),
            pltpu.VMEM((rows, voc), jnp.float32),
            pltpu.VMEM((rows, voc), jnp.bfloat16),
            pltpu.SemaphoreType.DMA((4,)),
        ]
        + ([pltpu.VMEM((width, voc), jnp.bfloat16), pltpu.SemaphoreType.DMA((CHUNKS,))] if streamed else []),
        input_output_aliases={} if filled is None else {count + 2: 0},
        compiler_params=pltpu.CompilerParams(vmem_limit_bytes=(52 if streamed else 8) * 1024 * 1024),
        cost_estimate=pl.CostEstimate(
            flops=2 * rows * width * voc, bytes_accessed=2 * width * (voc + rows), transcendentals=0
        ),
    )(*operands)


def merge(stats):
    stats = jnp.stack(stats)
    own_max = jnp.max(stats[:, 0], axis=0)
    peer_max = jnp.max(stats[:, 2], axis=0)
    own_scale = jnp.exp(stats[:, 0] - own_max)
    peer_scale = jnp.exp(stats[:, 2] - peer_max)
    (terms,) = tied(
        jnp.stack([stats[:, 1] * own_scale, stats[:, 3] * peer_scale, stats[:, 4], stats[:, 5] * peer_scale])
    )
    own_sum, peer_sum, target, cross = (terms[:, 0] + terms[:, 1]) + (terms[:, 2] + terms[:, 3])
    return jnp.stack([own_max, own_sum, peer_max, peer_sum, target, cross])


def wide(block):
    return block.astype(jnp.float32)


def narrow(block):
    return block.astype(jnp.bfloat16)


def sum_rows(grad_logits, matrix, later):
    voc = grad_logits.shape[1]
    width = matrix.shape[0] // 4
    at_x, at_z = bits(lax.axis_index("tx")), bits(lax.axis_index("tz"))
    rows = grad_logits.reshape(4, 4, 4, 8, voc)
    for axis in (1, 2):
        rows = jnp.concatenate([lax.slice_in_dim(rows, j, j + 1, axis=axis) for j in (0, 3, 1, 2)], axis=axis)
    rows = rows.reshape(4, 2, 2, 2, 2, 8, voc)
    dims = {"xa": (1, at_x[0], "tx", 1), "xb": (2, at_x[1], "tx", 3), "za": (3, at_z[0], "tz", 1), "zb": (4, at_z[1], "tz", 3)}
    orders = [("xa", "xb", "za", "zb"), ("xb", "xa", "zb", "za"), ("za", "zb", "xa", "xb"), ("zb", "za", "xb", "xa")]

    def product(block, q):
        columns = matrix[q * width : (q + 1) * width]
        out = lax.dot_general(
            block.reshape(-1, voc), columns, (((1,), (1,)), ((), ())), preferred_element_type=jnp.float32
        )
        return out.reshape(block.shape[:-1] + (width,))

    def split(block, name):
        at = dims[name][1]
        away = lax.dynamic_index_in_dim(block, 1 - at, 0, keepdims=False)
        return away, lax.dynamic_index_in_dim(block, at, 0, keepdims=False)

    def swap(block, name):
        axis, step = dims[name][2:]
        return lax.ppermute(block, axis, [(i, i ^ step) for i in range(4)])

    away, stay = [], []
    for q, order in enumerate(orders):
        turned_rows = jnp.transpose(rows, [dims[name][0] for name in order] + [0, 5, 6])
        one, other = split(turned_rows, order[0])
        away.append(narrow(product(*tied(one), q)))
        stay.append(other)
    *stay, away[3] = tied(*stay, away[3])
    came = [swap(away[q], orders[q][0]) for q in range(4)]
    kept = [product(stay[q], q) for q in range(4)]
    came[0], later = tied(came[0], later)
    for stage in range(1, 4):
        halves = [
            [k + wide(c) for k, c in zip(split(kept[q], orders[q][stage]), split(came[q], orders[q][stage]))]
            for q in range(4)
        ]
        came = [swap(narrow(halves[q][0]), orders[q][stage]) for q in range(4)]
        kept = [halves[q][1] for q in range(4)]
    state = [kept[q] + wide(came[q]) for q in range(4)]
    done = []
    for pair, first, second, steps in ((state[:2], NEAR, WRAP, (1, 3)), (state[2:], WRAP, NEAR, (3, 1))):
        block = jnp.concatenate(pair, axis=-1)
        came = swap_y(narrow(jnp.stack([block[first], block[FAR]])), (steps[0],) * 2)
        mine = block[OWN] + wide(came[0])
        came = swap_y(narrow(block[second] + wide(came[1])), (steps[1],) * 2)
        done.append(mine + wide(came))
    return done, later


def shard_stats(logits, peer_logits, hit):
    values, peer_values = wide(logits), wide(peer_logits)
    own_max = jnp.max(values, axis=-1)
    peer_max = jnp.max(peer_values, axis=-1)
    peer_exp = jnp.exp(peer_values - peer_max[:, None])
    return jnp.stack(
        [
            own_max,
            jnp.sum(jnp.exp(values - own_max[:, None]), axis=-1),
            peer_max,
            jnp.sum(peer_exp, axis=-1),
            jnp.sum(jnp.where(hit, values, 0.0), axis=-1),
            jnp.sum(peer_exp * (peer_values - values), axis=-1),
        ]
    )


def norm_backward_kernel(count, *refs):
    states_ref, gain_ref, out_ref = refs[count:]
    states = states_ref[...]
    width = states.shape[1]
    inverse = lax.rsqrt(jnp.sum(states * states, axis=-1, keepdims=True) / width + eps_norm)
    pieces, start = [], 0
    for ref in refs[:count]:
        columns = slice(start, start + ref.shape[1])
        pieces.append((ref[...] * gain_ref[:, columns], columns))
        start += ref.shape[1]
    inner = sum(jnp.sum(scaled * states[:, columns], axis=-1, keepdims=True) for scaled, columns in pieces) / width
    for scaled, columns in pieces:
        rows = narrow(inverse * (scaled - states[:, columns] * inverse * inverse * inner))
        for k in range(out_ref.shape[0]):
            out_ref[k, :, columns] = rows


def mean_loss(stats, weights):
    own_log = stats[0] + jnp.log(stats[1])
    peer_log = stats[2] + jnp.log(stats[3])
    per_token = own_log - stats[4] + kl_weight * (stats[5] / stats[3] - peer_log + own_log)
    sums = jnp.sum((weights * per_token).reshape(4, -1), axis=-1)
    total = (sums[OWN] + sums[NEAR]) + (sums[FAR] + sums[WRAP])
    return (total / jnp.sum(weights)).reshape((1,))


def local(hidden, gain, head, targets, lengths):
    block = hidden[0]
    gain_row = gain[0][None, :]
    matrix = head[0]
    group = block.shape[0]
    tokens = 4 * group
    voc_shard = matrix.shape[1]
    logits, ints = gather_logits(block, gain_row, matrix, jnp.concatenate([targets, lengths]))
    all_targets = jnp.concatenate([part[:group] for part in ints])
    all_lengths = jnp.concatenate([part[group:] for part in ints])
    peer_logits = lax.ppermute(logits, "peer", [(0, 1), (1, 0)])
    hit = all_targets[:, None] - lax.axis_index(("dp", "tx", "tz")) * voc_shard
    hit = hit == lax.broadcasted_iota(jnp.int32, (1, voc_shard), 1)
    stats = shard_stats(logits, peer_logits, hit)
    stats = merge(ring(stats, "tz"))
    stats = merge(ring(stats, "tx"))
    stats = ring(stats, "dp")
    stats = merge([stats[0]] + [turned(stats[s], s, 1) for s in (1, 2, 3)])
    own_log = stats[0] + jnp.log(stats[1])
    peer_log = stats[2] + jnp.log(stats[3])
    values, peer_values = wide(logits), wide(peer_logits)
    position = lax.broadcasted_iota(jnp.int32, (tokens // LEN, LEN), 1)
    weights = (position < all_lengths[:, None]).astype(jnp.float32).reshape(tokens)

    grad_logits = (
        loss_scale
        * weights[:, None]
        * (
            (1.0 + kl_weight) * jnp.exp(values - own_log[:, None])
            - hit.astype(jnp.float32)
            - kl_weight * jnp.exp(peer_values - peer_log[:, None])
        )
    ).astype(jnp.bfloat16)
    grad_normed, stats = sum_rows(grad_logits, matrix, stats)
    loss = mean_loss(stats, weights)

    own = lax.dynamic_slice_in_dim(block, lax.axis_index(("tx", "tz")) * 8, 8, axis=0)
    spread = pl.pallas_call(
        functools.partial(norm_backward_kernel, len(grad_normed)),
        out_shape=jax.ShapeDtypeStruct((16,) + own.shape, own.dtype),
        compiler_params=pltpu.CompilerParams(vmem_limit_bytes=16 * 1024 * 1024),
    )(*grad_normed, wide(own), gain_row)
    grad_hidden = lax.all_to_all(spread, ("tx", "tz"), split_axis=0, concat_axis=0, tiled=True)
    return (loss, grad_hidden.reshape((1,) + block.shape))


def solution(mesh):
    cube = Mesh(mesh.devices.reshape(2, 4, 4, 4), ALL)
    return jax.shard_map(
        local,
        mesh=cube,
        in_specs=(
            P("peer", "dp", None),
            P("peer", None),
            P("peer", None, ("dp", "tx", "tz")),
            P("dp"),
            P("dp"),
        ),
        out_specs=(P("peer"), P("peer", "dp", None)),
        check_vma=False,
    )
```

```python
import functools

import jax
import jax.numpy as jnp
from jax import lax
from jax.experimental import pallas as pl
from jax.experimental.pallas import tpu as pltpu
from jax.sharding import Mesh, PartitionSpec as P

LEN = 32
TILE = 128

kl_weight = 0.5
loss_scale = 64.0
eps_norm = 1e-06

ALL = ("peer", "dp", "tx", "tz")

OWN, NEAR, WRAP, FAR = range(4)
FLIP = {1: 1, 2: 3, 3: 2}


def permute(block, move):
    def index(core, y, x, z):
        return ((core * 4 + y) * 4 + x) * 4 + z

    places = [(c, y, x, z) for c in range(2) for y in range(4) for x in range(4) for z in range(4)]
    return lax.ppermute(block, ALL, [(index(*p), index(*move(*p))) for p in places])


def swap_u(block, step):
    return permute(block, lambda c, y, x, z: (c, y, x ^ step, z) if c == 0 else (c, y, x, z ^ step))


def swap_y(block, steps):
    return permute(block, lambda c, y, x, z: (c, y ^ steps[c], x, z))


def core():
    return lax.axis_index("peer")


def by_core(first, second):
    return jnp.where(core() == 0, first, second)


def bits(position):
    return (position ^ (position >> 1)) & 1, position >> 1


def parity():
    return (lax.axis_index("tx") + lax.axis_index("tz")) & 1


def tied(*blocks):
    return lax.optimization_barrier(blocks)


def ring(block, axis):
    near, wrap, far = [lax.ppermute(block, axis, [(i, i ^ s) for i in range(4)]) for s in (1, 3, 2)]
    return [block, near, far, wrap]


def turned(block, step, axis):
    size = block.shape[axis] // 4
    parts = [lax.slice_in_dim(block, p * size, (p + 1) * size, axis=axis) for p in range(4)]
    return jnp.concatenate([parts[p ^ FLIP[step]] for p in range(4)], axis=axis)


def gather_logits(block, gain_row, matrix, ints):
    half = block.shape[0] // 2
    tokens = 4 * block.shape[0]
    mine = lax.dynamic_slice_in_dim(block, parity() * half, half, axis=0)
    p = swap_y(mine, (1, 3))
    q = swap_y(mine, (3, 1))
    ints = ring(ints, "dp")
    logits = add_logits((block,), OWN_PLAN, gain_row, matrix, tokens)
    p, q, logits, *ints = tied(p, q, logits, *ints)
    far = swap_y(q, (1, 3))
    p_side, q_side = swap_u(p, 1), swap_u(q, 3)
    logits = add_logits((p, q), HELD_PLAN, gain_row, matrix, tokens, logits)
    far, logits = tied(far, logits)
    far_sides = [swap_u(far[: half // 2], 1), swap_u(far[half // 2 :], 3)]
    logits = add_logits((p_side, q_side), OTHER_PLAN, gain_row, matrix, tokens, logits)
    logits = add_logits((far, *far_sides), FAR_PLAN, gain_row, matrix, tokens, logits)
    return logits, [ints[s] for s in (0, 1, 3, 2)]


def make_kernel(count, loads, stores):
    def kernel(*refs):
        sources = refs[:count]
        gain_ref, head_ref = refs[count : count + 2]
        out_ref, rows, sums, total, block, sems = refs[-6:]
        width = rows.shape[1]
        held = parity() * 64
        p_first = 128 * (NEAR + core() * (WRAP - NEAR))
        q_first = 128 * (NEAR + WRAP) - p_first
        shift = {"all": 0, "held": held, "other": 64 - held}
        shift |= {"p held": p_first + held, "q held": q_first + held}
        shift |= {"p other": p_first + 64 - held, "q other": q_first + 64 - held}
        copies = []
        for source, start, length, target, kind in loads:
            to = pl.multiple_of(shift[kind] + target, 16)
            copies.append(
                pltpu.make_async_copy(
                    sources[source].at[pl.ds(start, length)], rows.at[pl.ds(to, length)], sems.at[len(copies)]
                )
            )
        for copy in copies:
            copy.start()
        for copy in copies:
            copy.wait()

        @pl.loop(0, rows.shape[0] // 16)
        def _(step):
            piece = pl.ds(pl.multiple_of(step * 16, 16), 16)
            lanes = jnp.zeros((16, TILE), jnp.float32)
            for c in range(0, width, TILE):
                states = rows[piece, c : c + TILE].astype(jnp.float32)
                lanes += states * states
            sums[piece, :] = lanes

        mean = jnp.sum(sums[...], axis=-1, keepdims=True) / width
        sums[...] = jnp.broadcast_to(lax.rsqrt(mean + eps_norm), sums.shape)

        @pl.loop(0, rows.shape[0] // 16)
        def _(step):
            piece = pl.ds(pl.multiple_of(step * 16, 16), 16)
            inverse = sums[piece, :]
            for c in range(0, width, TILE):
                states = rows[piece, c : c + TILE].astype(jnp.float32)
                rows[piece, c : c + TILE] = (states * inverse * gain_ref[:, c : c + TILE]).astype(jnp.bfloat16)

        depth = 1024
        for c in range(0, width, depth):
            part = jnp.dot(rows[:, c : c + depth], head_ref[c : c + depth, :], preferred_element_type=jnp.float32)
            if c == 0:
                total[...] = part
            elif c + depth < width:
                total[...] += part
            else:
                block[...] = (total[...] + part).astype(jnp.bfloat16)
        copies = []
        for start, length, target, kind in stores:
            to = pl.multiple_of(shift[kind] + target, 16)
            copies.append(
                pltpu.make_async_copy(
                    block.at[pl.ds(start, length)], out_ref.at[pl.ds(to, length)], sems.at[len(copies)]
                )
            )
        for copy in copies:
            copy.start()
        for copy in copies:
            copy.wait()

    return kernel


OWN_PLAN = [(0, 0, 128, 0, "all")], [(0, 128, 0, "all")]
HELD_PLAN = [(0, 0, 64, 0, "all"), (1, 0, 64, 64, "all")], [(0, 64, 0, "p held"), (64, 64, 0, "q held")]
OTHER_PLAN = [(0, 0, 64, 0, "all"), (1, 0, 64, 64, "all")], [(0, 64, 0, "p other"), (64, 64, 0, "q other")]
FAR_PLAN = (
    [(0, 0, 64, 0, "held")] + [(1 + k, 0, 32, 32 * k, "other") for k in range(2)],
    [(0, 128, FAR * 128, "all")],
)


def add_logits(sources, plan, gain_row, matrix, tokens, filled=None):
    width, voc = matrix.shape
    anywhere = pl.BlockSpec(memory_space=pl.ANY)
    count = len(sources)
    rows = sum(piece[2] for piece in plan[0])
    operands = [*sources, gain_row, matrix] + ([] if filled is None else [filled])
    return pl.pallas_call(
        make_kernel(count, *plan),
        out_shape=jax.ShapeDtypeStruct((tokens, voc), jnp.bfloat16),
        in_specs=[anywhere] * count
        + [pl.BlockSpec(memory_space=pltpu.VMEM)] * 2
        + ([] if filled is None else [anywhere]),
        out_specs=anywhere,
        scratch_shapes=[
            pltpu.VMEM((rows, width), jnp.bfloat16),
            pltpu.VMEM((rows, TILE), jnp.float32),
            pltpu.VMEM((rows, voc), jnp.float32),
            pltpu.VMEM((rows, voc), jnp.bfloat16),
            pltpu.SemaphoreType.DMA((4,)),
        ],
        input_output_aliases={} if filled is None else {count + 2: 0},
        compiler_params=pltpu.CompilerParams(vmem_limit_bytes=8 * 1024 * 1024),
        cost_estimate=pl.CostEstimate(
            flops=2 * rows * width * voc, bytes_accessed=2 * width * (voc + rows), transcendentals=0
        ),
    )(*operands)


def merge(stats):
    stats = jnp.stack(stats)
    own_max = jnp.max(stats[:, 0], axis=0)
    peer_max = jnp.max(stats[:, 2], axis=0)
    own_scale = jnp.exp(stats[:, 0] - own_max)
    peer_scale = jnp.exp(stats[:, 2] - peer_max)
    (terms,) = tied(
        jnp.stack([stats[:, 1] * own_scale, stats[:, 3] * peer_scale, stats[:, 4], stats[:, 5] * peer_scale])
    )
    own_sum, peer_sum, target, cross = (terms[:, 0] + terms[:, 1]) + (terms[:, 2] + terms[:, 3])
    return jnp.stack([own_max, own_sum, peer_max, peer_sum, target, cross])


def wide(block):
    return block.astype(jnp.float32)


def narrow(block):
    return block.astype(jnp.bfloat16)


def sum_rows(grad_logits, matrix, later):
    voc = grad_logits.shape[1]
    width = matrix.shape[0] // 4
    at_x, at_z = bits(lax.axis_index("tx")), bits(lax.axis_index("tz"))
    rows = grad_logits.reshape(4, 4, 4, 8, voc)
    for axis in (1, 2):
        rows = jnp.concatenate([lax.slice_in_dim(rows, j, j + 1, axis=axis) for j in (0, 3, 1, 2)], axis=axis)
    rows = rows.reshape(4, 2, 2, 2, 2, 8, voc)
    dims = {"xa": (1, at_x[0], "tx", 1), "xb": (2, at_x[1], "tx", 3), "za": (3, at_z[0], "tz", 1), "zb": (4, at_z[1], "tz", 3)}
    orders = [("xa", "xb", "za", "zb"), ("xb", "xa", "zb", "za"), ("za", "zb", "xa", "xb"), ("zb", "za", "xb", "xa")]

    def product(block, q):
        columns = matrix[q * width : (q + 1) * width]
        out = lax.dot_general(
            block.reshape(-1, voc), columns, (((1,), (1,)), ((), ())), preferred_element_type=jnp.float32
        )
        return out.reshape(block.shape[:-1] + (width,))

    def split(block, name):
        at = dims[name][1]
        away = lax.dynamic_index_in_dim(block, 1 - at, 0, keepdims=False)
        return away, lax.dynamic_index_in_dim(block, at, 0, keepdims=False)

    def swap(block, name):
        axis, step = dims[name][2:]
        return lax.ppermute(block, axis, [(i, i ^ step) for i in range(4)])

    sent, stay = [], []
    for q, order in enumerate(orders):
        turned_rows = jnp.transpose(rows, [dims[name][0] for name in order] + [0, 5, 6])
        one, other = split(turned_rows, order[0])
        sent.append(product(*tied(one), q))
        stay.append(split(other, order[1]))
    came = [swap(narrow(sent[q]), orders[q][0]) for q in range(4)]
    came[0], later = tied(came[0], later)
    kept = []
    for q, order in enumerate(orders):
        pairs = zip(stay[q], split(came[q], order[1]))
        one, other = [product(block, q) + wide(part) for block, part in pairs]
        came[q] = swap(narrow(one), order[1])
        kept.append(other)
    for stage in range(2, 4):
        halves = [
            [k + wide(c) for k, c in zip(split(kept[q], orders[q][stage]), split(came[q], orders[q][stage]))]
            for q in range(4)
        ]
        came = [swap(narrow(halves[q][0]), orders[q][stage]) for q in range(4)]
        kept = [halves[q][1] for q in range(4)]
    state = [kept[q] + wide(came[q]) for q in range(4)]
    done = []
    for pair, first, second, steps in ((state[:2], NEAR, WRAP, (1, 3)), (state[2:], WRAP, NEAR, (3, 1))):
        block = jnp.concatenate(pair, axis=-1)
        came = swap_y(narrow(jnp.stack([block[first], block[FAR]])), (steps[0],) * 2)
        mine = block[OWN] + wide(came[0])
        came = swap_y(narrow(block[second] + wide(came[1])), (steps[1],) * 2)
        done.append(mine + wide(came))
    return done, later


def shard_stats(logits, peer_logits, hit):
    values, peer_values = wide(logits), wide(peer_logits)
    own_max = jnp.max(values, axis=-1)
    peer_max = jnp.max(peer_values, axis=-1)
    peer_exp = jnp.exp(peer_values - peer_max[:, None])
    return jnp.stack(
        [
            own_max,
            jnp.sum(jnp.exp(values - own_max[:, None]), axis=-1),
            peer_max,
            jnp.sum(peer_exp, axis=-1),
            jnp.sum(jnp.where(hit, values, 0.0), axis=-1),
            jnp.sum(peer_exp * (peer_values - values), axis=-1),
        ]
    )


def norm_backward_kernel(count, *refs):
    states_ref, gain_ref, out_ref = refs[count:]
    states = states_ref[...]
    width = states.shape[1]
    inverse = lax.rsqrt(jnp.sum(states * states, axis=-1, keepdims=True) / width + eps_norm)
    pieces, start = [], 0
    for ref in refs[:count]:
        columns = slice(start, start + ref.shape[1])
        pieces.append((ref[...] * gain_ref[:, columns], columns))
        start += ref.shape[1]
    inner = sum(jnp.sum(scaled * states[:, columns], axis=-1, keepdims=True) for scaled, columns in pieces) / width
    for scaled, columns in pieces:
        rows = narrow(inverse * (scaled - states[:, columns] * inverse * inverse * inner))
        for k in range(out_ref.shape[0]):
            out_ref[k, :, columns] = rows


def mean_loss(stats, weights):
    own_log = stats[0] + jnp.log(stats[1])
    peer_log = stats[2] + jnp.log(stats[3])
    per_token = own_log - stats[4] + kl_weight * (stats[5] / stats[3] - peer_log + own_log)
    sums = jnp.sum((weights * per_token).reshape(4, -1), axis=-1)
    total = (sums[OWN] + sums[NEAR]) + (sums[FAR] + sums[WRAP])
    return (total / jnp.sum(weights)).reshape((1,))


def local(hidden, gain, head, targets, lengths):
    block = hidden[0]
    gain_row = gain[0][None, :]
    matrix = head[0]
    group = block.shape[0]
    tokens = 4 * group
    voc_shard = matrix.shape[1]
    logits, ints = gather_logits(block, gain_row, matrix, jnp.concatenate([targets, lengths]))
    all_targets = jnp.concatenate([part[:group] for part in ints])
    all_lengths = jnp.concatenate([part[group:] for part in ints])
    peer_logits = lax.ppermute(logits, "peer", [(0, 1), (1, 0)])
    hit = all_targets[:, None] - lax.axis_index(("dp", "tx", "tz")) * voc_shard
    hit = hit == lax.broadcasted_iota(jnp.int32, (1, voc_shard), 1)
    stats = shard_stats(logits, peer_logits, hit)
    stats = merge(ring(stats, "tz"))
    stats = merge(ring(stats, "tx"))
    stats = ring(stats, "dp")
    stats = merge([stats[0]] + [turned(stats[s], s, 1) for s in (1, 2, 3)])
    own_log = stats[0] + jnp.log(stats[1])
    peer_log = stats[2] + jnp.log(stats[3])
    values, peer_values = wide(logits), wide(peer_logits)
    position = lax.broadcasted_iota(jnp.int32, (tokens // LEN, LEN), 1)
    weights = (position < all_lengths[:, None]).astype(jnp.float32).reshape(tokens)

    grad_logits = (
        loss_scale
        * weights[:, None]
        * (
            (1.0 + kl_weight) * jnp.exp(values - own_log[:, None])
            - hit.astype(jnp.float32)
            - kl_weight * jnp.exp(peer_values - peer_log[:, None])
        )
    ).astype(jnp.bfloat16)
    grad_normed, stats = sum_rows(grad_logits, matrix, stats)
    loss = mean_loss(stats, weights)

    own = lax.dynamic_slice_in_dim(block, lax.axis_index(("tx", "tz")) * 8, 8, axis=0)
    spread = pl.pallas_call(
        functools.partial(norm_backward_kernel, len(grad_normed)),
        out_shape=jax.ShapeDtypeStruct((16,) + own.shape, own.dtype),
        compiler_params=pltpu.CompilerParams(vmem_limit_bytes=16 * 1024 * 1024),
    )(*grad_normed, wide(own), gain_row)
    grad_hidden = lax.all_to_all(spread, ("tx", "tz"), split_axis=0, concat_axis=0, tiled=True)
    return (loss, grad_hidden.reshape((1,) + block.shape))


def solution(mesh):
    cube = Mesh(mesh.devices.reshape(2, 4, 4, 4), ALL)
    return jax.shard_map(
        local,
        mesh=cube,
        in_specs=(
            P("peer", "dp", None),
            P("peer", None),
            P("peer", None, ("dp", "tx", "tz")),
            P("dp"),
            P("dp"),
        ),
        out_specs=(P("peer"), P("peer", "dp", None)),
        check_vma=False,
    )
```

```python
import functools

import jax
import jax.numpy as jnp
from jax import lax
from jax.experimental import pallas as pl
from jax.experimental.pallas import tpu as pltpu
from jax.sharding import Mesh, PartitionSpec as P

LEN = 32
TILE = 128

kl_weight = 0.5
loss_scale = 64.0
eps_norm = 1e-06

ALL = ("peer", "dp", "tx", "tz")

OWN, NEAR, WRAP, FAR = range(4)
FLIP = {1: 1, 2: 3, 3: 2}


def permute(block, move):
    def index(core, y, x, z):
        return ((core * 4 + y) * 4 + x) * 4 + z

    places = [(c, y, x, z) for c in range(2) for y in range(4) for x in range(4) for z in range(4)]
    return lax.ppermute(block, ALL, [(index(*p), index(*move(*p))) for p in places])


def swap_u(block, step):
    return permute(block, lambda c, y, x, z: (c, y, x ^ step, z) if c == 0 else (c, y, x, z ^ step))


def swap_y(block, steps):
    return permute(block, lambda c, y, x, z: (c, y ^ steps[c], x, z))


def core():
    return lax.axis_index("peer")


def by_core(first, second):
    return jnp.where(core() == 0, first, second)


def bits(position):
    return (position ^ (position >> 1)) & 1, position >> 1


def parity():
    return (lax.axis_index("tx") + lax.axis_index("tz")) & 1


def tied(*blocks):
    return lax.optimization_barrier(blocks)


def ring(block, axis):
    far, near, wrap = [lax.ppermute(block, axis, [(i, i ^ s) for i in range(4)]) for s in (2, 1, 3)]
    return [block, near, far, wrap]


def turned(block, step, axis):
    size = block.shape[axis] // 4
    parts = [lax.slice_in_dim(block, p * size, (p + 1) * size, axis=axis) for p in range(4)]
    return jnp.concatenate([parts[p ^ FLIP[step]] for p in range(4)], axis=axis)


def gather_logits(block, gain_row, matrix, ints):
    half = block.shape[0] // 2
    tokens = 4 * block.shape[0]
    mine = lax.dynamic_slice_in_dim(block, parity() * half, half, axis=0)
    p = swap_y(mine, (1, 3))
    q = swap_y(mine, (3, 1))
    ints = ring(ints, "dp")
    logits = add_logits((block,), OWN_PLAN, gain_row, matrix, tokens)
    p, q, logits, *ints = tied(p, q, logits, *ints)
    far = swap_y(q, (1, 3))
    p_side, q_side = swap_u(p, 1), swap_u(q, 3)
    logits = add_logits((p, q), HELD_PLAN, gain_row, matrix, tokens, logits)
    far, logits = tied(far, logits)
    far_sides = [swap_u(far[: half // 2], 1), swap_u(far[half // 2 :], 3)]
    logits = add_logits((p_side, q_side), OTHER_PLAN, gain_row, matrix, tokens, logits)
    logits = add_logits((far, *far_sides), FAR_PLAN, gain_row, matrix, tokens, logits)
    return logits, [ints[s] for s in (0, 1, 3, 2)]


def make_kernel(count, loads, stores):
    def kernel(*refs):
        sources = refs[:count]
        gain_ref, head_ref = refs[count : count + 2]
        out_ref, rows, sums, total, block, sems = refs[-6:]
        width = rows.shape[1]
        held = parity() * 64
        p_first = 128 * (NEAR + core() * (WRAP - NEAR))
        q_first = 128 * (NEAR + WRAP) - p_first
        shift = {"all": 0, "held": held, "other": 64 - held}
        shift |= {"p held": p_first + held, "q held": q_first + held}
        shift |= {"p other": p_first + 64 - held, "q other": q_first + 64 - held}
        copies = []
        for source, start, length, target, kind in loads:
            to = pl.multiple_of(shift[kind] + target, 16)
            copies.append(
                pltpu.make_async_copy(
                    sources[source].at[pl.ds(start, length)], rows.at[pl.ds(to, length)], sems.at[len(copies)]
                )
            )
        for copy in copies:
            copy.start()
        for copy in copies:
            copy.wait()

        @pl.loop(0, rows.shape[0] // 16)
        def _(step):
            piece = pl.ds(pl.multiple_of(step * 16, 16), 16)
            lanes = jnp.zeros((16, TILE), jnp.float32)
            for c in range(0, width, TILE):
                states = rows[piece, c : c + TILE].astype(jnp.float32)
                lanes += states * states
            sums[piece, :] = lanes

        mean = jnp.sum(sums[...], axis=-1, keepdims=True) / width
        sums[...] = jnp.broadcast_to(lax.rsqrt(mean + eps_norm), sums.shape)

        @pl.loop(0, rows.shape[0] // 16)
        def _(step):
            piece = pl.ds(pl.multiple_of(step * 16, 16), 16)
            inverse = sums[piece, :]
            for c in range(0, width, TILE):
                states = rows[piece, c : c + TILE].astype(jnp.float32)
                rows[piece, c : c + TILE] = (states * inverse * gain_ref[:, c : c + TILE]).astype(jnp.bfloat16)

        depth = 1024
        for c in range(0, width, depth):
            part = jnp.dot(rows[:, c : c + depth], head_ref[c : c + depth, :], preferred_element_type=jnp.float32)
            if c == 0:
                total[...] = part
            elif c + depth < width:
                total[...] += part
            else:
                block[...] = (total[...] + part).astype(jnp.bfloat16)
        copies = []
        for start, length, target, kind in stores:
            to = pl.multiple_of(shift[kind] + target, 16)
            copies.append(
                pltpu.make_async_copy(
                    block.at[pl.ds(start, length)], out_ref.at[pl.ds(to, length)], sems.at[len(copies)]
                )
            )
        for copy in copies:
            copy.start()
        for copy in copies:
            copy.wait()

    return kernel


OWN_PLAN = [(0, 0, 128, 0, "all")], [(0, 128, 0, "all")]
HELD_PLAN = [(0, 0, 64, 0, "all"), (1, 0, 64, 64, "all")], [(0, 64, 0, "p held"), (64, 64, 0, "q held")]
OTHER_PLAN = [(0, 0, 64, 0, "all"), (1, 0, 64, 64, "all")], [(0, 64, 0, "p other"), (64, 64, 0, "q other")]
FAR_PLAN = (
    [(0, 0, 64, 0, "held")] + [(1 + k, 0, 32, 32 * k, "other") for k in range(2)],
    [(0, 128, FAR * 128, "all")],
)


def add_logits(sources, plan, gain_row, matrix, tokens, filled=None):
    width, voc = matrix.shape
    anywhere = pl.BlockSpec(memory_space=pl.ANY)
    count = len(sources)
    rows = sum(piece[2] for piece in plan[0])
    operands = [*sources, gain_row, matrix] + ([] if filled is None else [filled])
    return pl.pallas_call(
        make_kernel(count, *plan),
        out_shape=jax.ShapeDtypeStruct((tokens, voc), jnp.bfloat16),
        in_specs=[anywhere] * count
        + [pl.BlockSpec(memory_space=pltpu.VMEM)] * 2
        + ([] if filled is None else [anywhere]),
        out_specs=anywhere,
        scratch_shapes=[
            pltpu.VMEM((rows, width), jnp.bfloat16),
            pltpu.VMEM((rows, TILE), jnp.float32),
            pltpu.VMEM((rows, voc), jnp.float32),
            pltpu.VMEM((rows, voc), jnp.bfloat16),
            pltpu.SemaphoreType.DMA((4,)),
        ],
        input_output_aliases={} if filled is None else {count + 2: 0},
        compiler_params=pltpu.CompilerParams(vmem_limit_bytes=8 * 1024 * 1024),
        cost_estimate=pl.CostEstimate(
            flops=2 * rows * width * voc, bytes_accessed=2 * width * (voc + rows), transcendentals=0
        ),
    )(*operands)


def merge(stats):
    stats = jnp.stack(stats)
    own_max = jnp.max(stats[:, 0], axis=0)
    peer_max = jnp.max(stats[:, 2], axis=0)
    own_scale = jnp.exp(stats[:, 0] - own_max)
    peer_scale = jnp.exp(stats[:, 2] - peer_max)
    (terms,) = tied(
        jnp.stack([stats[:, 1] * own_scale, stats[:, 3] * peer_scale, stats[:, 4], stats[:, 5] * peer_scale])
    )
    own_sum, peer_sum, target, cross = (terms[:, 0] + terms[:, 1]) + (terms[:, 2] + terms[:, 3])
    return jnp.stack([own_max, own_sum, peer_max, peer_sum, target, cross])


def wide(block):
    return block.astype(jnp.float32)


def narrow(block):
    return block.astype(jnp.bfloat16)


def sum_rows(grad_logits, matrix, later):
    voc = grad_logits.shape[1]
    width = matrix.shape[0] // 4
    at_x, at_z = bits(lax.axis_index("tx")), bits(lax.axis_index("tz"))
    rows = grad_logits.reshape(4, 4, 4, 8, voc)
    for axis in (1, 2):
        rows = jnp.concatenate([lax.slice_in_dim(rows, j, j + 1, axis=axis) for j in (0, 3, 1, 2)], axis=axis)
    rows = rows.reshape(4, 2, 2, 2, 2, 8, voc)
    dims = {"xa": (1, at_x[0], "tx", 1), "xb": (2, at_x[1], "tx", 3), "za": (3, at_z[0], "tz", 1), "zb": (4, at_z[1], "tz", 3)}
    orders = [("xa", "xb", "za", "zb"), ("xb", "xa", "zb", "za"), ("za", "zb", "xa", "xb"), ("zb", "za", "xb", "xa")]

    def product(block, q):
        columns = matrix[q * width : (q + 1) * width]
        out = lax.dot_general(
            block.reshape(-1, voc), columns, (((1,), (1,)), ((), ())), preferred_element_type=jnp.float32
        )
        return out.reshape(block.shape[:-1] + (width,))

    def split(block, name):
        at = dims[name][1]
        away = lax.dynamic_index_in_dim(block, 1 - at, 0, keepdims=False)
        return away, lax.dynamic_index_in_dim(block, at, 0, keepdims=False)

    def swap(block, name):
        axis, step = dims[name][2:]
        return lax.ppermute(block, axis, [(i, i ^ step) for i in range(4)])

    sent, stay = [], []
    for q, order in enumerate(orders):
        turned_rows = jnp.transpose(rows, [dims[name][0] for name in order] + [0, 5, 6])
        one, other = split(turned_rows, order[0])
        sent.append(product(*tied(one), q))
        stay.append(split(other, order[1]))
    came = [swap(narrow(sent[q]), orders[q][0]) for q in range(4)]
    came[0], later = tied(came[0], later)
    kept = []
    for q, order in enumerate(orders):
        one, other = [product(part, q) + wide(block) for part, block in zip(stay[q], split(came[q], order[1]))]
        came[q] = swap(narrow(one), order[1])
        kept.append(other)
    for stage in range(2, 4):
        halves = [
            [k + wide(c) for k, c in zip(split(kept[q], orders[q][stage]), split(came[q], orders[q][stage]))]
            for q in range(4)
        ]
        came = [swap(narrow(halves[q][0]), orders[q][stage]) for q in range(4)]
        kept = [halves[q][1] for q in range(4)]
    state = [kept[q] + wide(came[q]) for q in range(4)]
    block = jnp.concatenate(state, axis=-1)
    first, second = by_core(block[NEAR], block[WRAP]), by_core(block[WRAP], block[NEAR])
    came = swap_y(narrow(jnp.stack([first, block[FAR]])), (1, 3))
    mine, rest = block[OWN] + wide(came[0]), second + wide(came[1])
    return [mine + wide(swap_y(narrow(rest), (3, 1)))], later


def shard_stats(logits, peer_logits, hit):
    values = wide(logits)
    own_max = jnp.max(values, axis=-1)
    own_sum = jnp.sum(jnp.exp(values - own_max[:, None]), axis=-1)
    target = jnp.sum(jnp.where(hit, values, 0.0), axis=-1)
    own_max, own_sum, target, peer_logits = tied(own_max, own_sum, target, peer_logits)
    peer_values = wide(peer_logits)
    peer_max = jnp.max(peer_values, axis=-1)
    peer_exp = jnp.exp(peer_values - peer_max[:, None])
    peer_sum = jnp.sum(peer_exp, axis=-1)
    cross = jnp.sum(peer_exp * (peer_values - values), axis=-1)
    return jnp.stack([own_max, own_sum, peer_max, peer_sum, target, cross]), peer_logits


def norm_backward_kernel(count, *refs):
    states_ref, gain_ref, out_ref = refs[count:]
    states = states_ref[...]
    width = states.shape[1]
    inverse = lax.rsqrt(jnp.sum(states * states, axis=-1, keepdims=True) / width + eps_norm)
    pieces, start = [], 0
    for ref in refs[:count]:
        columns = slice(start, start + ref.shape[1])
        pieces.append((ref[...] * gain_ref[:, columns], columns))
        start += ref.shape[1]
    inner = sum(jnp.sum(scaled * states[:, columns], axis=-1, keepdims=True) for scaled, columns in pieces) / width
    for scaled, columns in pieces:
        rows = narrow(inverse * (scaled - states[:, columns] * inverse * inverse * inner))
        for k in range(out_ref.shape[0]):
            out_ref[k, :, columns] = rows


def mean_loss(stats, weights):
    own_log = stats[0] + jnp.log(stats[1])
    peer_log = stats[2] + jnp.log(stats[3])
    per_token = own_log - stats[4] + kl_weight * (stats[5] / stats[3] - peer_log + own_log)
    sums = jnp.sum((weights * per_token).reshape(4, -1), axis=-1)
    total = (sums[OWN] + sums[NEAR]) + (sums[FAR] + sums[WRAP])
    return (total / jnp.sum(weights)).reshape((1,))


def local(hidden, gain, head, targets, lengths):
    block = hidden[0]
    gain_row = gain[0][None, :]
    matrix = head[0]
    group = block.shape[0]
    tokens = 4 * group
    voc_shard = matrix.shape[1]
    logits, ints = gather_logits(block, gain_row, matrix, jnp.concatenate([targets, lengths]))
    all_targets = jnp.concatenate([part[:group] for part in ints])
    all_lengths = jnp.concatenate([part[group:] for part in ints])
    peer_logits = lax.ppermute(logits, "peer", [(0, 1), (1, 0)])
    hit = all_targets[:, None] - lax.axis_index(("dp", "tx", "tz")) * voc_shard
    hit = hit == lax.broadcasted_iota(jnp.int32, (1, voc_shard), 1)
    stats, peer_logits = shard_stats(logits, peer_logits, hit)
    stats = merge(ring(stats, "tz"))
    stats = merge(ring(stats, "tx"))
    stats = ring(stats, "dp")
    stats = merge([stats[0]] + [turned(stats[s], s, 1) for s in (1, 2, 3)])
    own_log = stats[0] + jnp.log(stats[1])
    peer_log = stats[2] + jnp.log(stats[3])
    values, peer_values = wide(logits), wide(peer_logits)
    position = lax.broadcasted_iota(jnp.int32, (tokens // LEN, LEN), 1)
    weights = (position < all_lengths[:, None]).astype(jnp.float32).reshape(tokens)

    grad_logits = (
        loss_scale
        * weights[:, None]
        * (
            (1.0 + kl_weight) * jnp.exp(values - own_log[:, None])
            - hit.astype(jnp.float32)
            - kl_weight * jnp.exp(peer_values - peer_log[:, None])
        )
    ).astype(jnp.bfloat16)
    grad_normed, stats = sum_rows(grad_logits, matrix, stats)
    loss = mean_loss(stats, weights)

    own = lax.dynamic_slice_in_dim(block, lax.axis_index(("tx", "tz")) * 8, 8, axis=0)
    spread = pl.pallas_call(
        functools.partial(norm_backward_kernel, len(grad_normed)),
        out_shape=jax.ShapeDtypeStruct((16,) + own.shape, own.dtype),
        compiler_params=pltpu.CompilerParams(vmem_limit_bytes=16 * 1024 * 1024),
    )(*grad_normed, wide(own), gain_row)
    grad_hidden = lax.all_to_all(spread, ("tx", "tz"), split_axis=0, concat_axis=0, tiled=True)
    return (loss, grad_hidden.reshape((1,) + block.shape))


def solution(mesh):
    cube = Mesh(mesh.devices.reshape(2, 4, 4, 4), ALL)
    return jax.shard_map(
        local,
        mesh=cube,
        in_specs=(
            P("peer", "dp", None),
            P("peer", None),
            P("peer", None, ("dp", "tx", "tz")),
            P("dp"),
            P("dp"),
        ),
        out_specs=(P("peer"), P("peer", "dp", None)),
        check_vma=False,
    )
```

```python
import functools

import jax
import jax.numpy as jnp
from jax import lax
from jax.experimental import pallas as pl
from jax.experimental.pallas import tpu as pltpu
from jax.sharding import Mesh, PartitionSpec as P

LEN = 32
TILE = 128

kl_weight = 0.5
loss_scale = 64.0
eps_norm = 1e-06

LOWEST = -3.4e38

ALL = ("peer", "dp", "tx", "tz")

OWN, NEAR, WRAP, FAR = range(4)
FLIP = {1: 1, 2: 3, 3: 2}


def permute(block, move):
    def index(core, y, x, z):
        return ((core * 4 + y) * 4 + x) * 4 + z

    places = [(c, y, x, z) for c in range(2) for y in range(4) for x in range(4) for z in range(4)]
    return lax.ppermute(block, ALL, [(index(*p), index(*move(*p))) for p in places])


def swap_u(block, step):
    return permute(block, lambda c, y, x, z: (c, y, x ^ step, z) if c == 0 else (c, y, x, z ^ step))


def swap_y(block, steps):
    return permute(block, lambda c, y, x, z: (c, y ^ steps[c], x, z))


def core():
    return lax.axis_index("peer")


def by_core(first, second):
    return jnp.where(core() == 0, first, second)


def bits(position):
    return (position ^ (position >> 1)) & 1, position >> 1


def parity():
    return (lax.axis_index("tx") + lax.axis_index("tz")) & 1


def tied(*blocks):
    return lax.optimization_barrier(blocks)


def ring(block, axis, prepare=lambda block, step: block):
    far, near, wrap = [
        lax.ppermute(prepare(block, step), axis, [(i, i ^ step) for i in range(4)]) for step in (2, 1, 3)
    ]
    return [block, near, far, wrap]


def turned(block, step, axis):
    size = block.shape[axis] // 4
    parts = [lax.slice_in_dim(block, p * size, (p + 1) * size, axis=axis) for p in range(4)]
    return jnp.concatenate([parts[p ^ FLIP[step]] for p in range(4)], axis=axis)


def gather_logits(block, gain_row, matrix, ints):
    half = block.shape[0] // 2
    tokens = 4 * block.shape[0]
    mine = lax.dynamic_slice_in_dim(block, parity() * half, half, axis=0)
    p = swap_y(mine, (1, 3))
    q = swap_y(mine, (3, 1))
    ints = ring(ints, "dp")
    logits = add_logits((block,), OWN_PLAN, gain_row, matrix, tokens)
    p, q, logits, *ints = tied(p, q, logits, *ints)
    far = swap_y(q, (1, 3))
    p_side, q_side = swap_u(p, 1), swap_u(q, 3)
    logits = add_logits((p, q), HELD_PLAN, gain_row, matrix, tokens, logits)
    far, logits = tied(far, logits)
    far_sides = [swap_u(far[: half // 2], 1), swap_u(far[half // 2 :], 3)]
    logits = add_logits((p_side, q_side), OTHER_PLAN, gain_row, matrix, tokens, logits)
    logits = add_logits((far, *far_sides), FAR_PLAN, gain_row, matrix, tokens, logits)
    return logits, [ints[s] for s in (0, 1, 3, 2)]


def make_kernel(count, loads, stores):
    def kernel(*refs):
        sources = refs[:count]
        gain_ref, head_ref = refs[count : count + 2]
        out_ref, rows, sums, total, block, sems = refs[-6:]
        width = rows.shape[1]
        held = parity() * 64
        p_first = 128 * (NEAR + core() * (WRAP - NEAR))
        q_first = 128 * (NEAR + WRAP) - p_first
        shift = {"all": 0, "held": held, "other": 64 - held}
        shift |= {"p held": p_first + held, "q held": q_first + held}
        shift |= {"p other": p_first + 64 - held, "q other": q_first + 64 - held}
        copies = []
        for source, start, length, target, kind in loads:
            to = pl.multiple_of(shift[kind] + target, 16)
            copies.append(
                pltpu.make_async_copy(
                    sources[source].at[pl.ds(start, length)], rows.at[pl.ds(to, length)], sems.at[len(copies)]
                )
            )
        for copy in copies:
            copy.start()
        for copy in copies:
            copy.wait()

        @pl.loop(0, rows.shape[0] // 16)
        def _(step):
            piece = pl.ds(pl.multiple_of(step * 16, 16), 16)
            lanes = jnp.zeros((16, TILE), jnp.float32)
            for c in range(0, width, TILE):
                states = rows[piece, c : c + TILE].astype(jnp.float32)
                lanes += states * states
            sums[piece, :] = lanes

        mean = jnp.sum(sums[...], axis=-1, keepdims=True) / width
        sums[...] = jnp.broadcast_to(lax.rsqrt(mean + eps_norm), sums.shape)

        @pl.loop(0, rows.shape[0] // 16)
        def _(step):
            piece = pl.ds(pl.multiple_of(step * 16, 16), 16)
            inverse = sums[piece, :]
            for c in range(0, width, TILE):
                states = rows[piece, c : c + TILE].astype(jnp.float32)
                rows[piece, c : c + TILE] = (states * inverse * gain_ref[:, c : c + TILE]).astype(jnp.bfloat16)

        depth = 1024
        for c in range(0, width, depth):
            part = jnp.dot(rows[:, c : c + depth], head_ref[c : c + depth, :], preferred_element_type=jnp.float32)
            if c == 0:
                total[...] = part
            elif c + depth < width:
                total[...] += part
            else:
                block[...] = (total[...] + part).astype(jnp.bfloat16)
        copies = []
        for start, length, target, kind in stores:
            to = pl.multiple_of(shift[kind] + target, 16)
            copies.append(
                pltpu.make_async_copy(
                    block.at[pl.ds(start, length)], out_ref.at[pl.ds(to, length)], sems.at[len(copies)]
                )
            )
        for copy in copies:
            copy.start()
        for copy in copies:
            copy.wait()

    return kernel


OWN_PLAN = [(0, 0, 128, 0, "all")], [(0, 128, 0, "all")]
HELD_PLAN = [(0, 0, 64, 0, "all"), (1, 0, 64, 64, "all")], [(0, 64, 0, "p held"), (64, 64, 0, "q held")]
OTHER_PLAN = [(0, 0, 64, 0, "all"), (1, 0, 64, 64, "all")], [(0, 64, 0, "p other"), (64, 64, 0, "q other")]
FAR_PLAN = (
    [(0, 0, 64, 0, "held")] + [(1 + k, 0, 32, 32 * k, "other") for k in range(2)],
    [(0, 128, FAR * 128, "all")],
)


def add_logits(sources, plan, gain_row, matrix, tokens, filled=None):
    width, voc = matrix.shape
    anywhere = pl.BlockSpec(memory_space=pl.ANY)
    count = len(sources)
    rows = sum(piece[2] for piece in plan[0])
    operands = [*sources, gain_row, matrix] + ([] if filled is None else [filled])
    return pl.pallas_call(
        make_kernel(count, *plan),
        out_shape=jax.ShapeDtypeStruct((tokens, voc), jnp.bfloat16),
        in_specs=[anywhere] * count
        + [pl.BlockSpec(memory_space=pltpu.VMEM)] * 2
        + ([] if filled is None else [anywhere]),
        out_specs=anywhere,
        scratch_shapes=[
            pltpu.VMEM((rows, width), jnp.bfloat16),
            pltpu.VMEM((rows, TILE), jnp.float32),
            pltpu.VMEM((rows, voc), jnp.float32),
            pltpu.VMEM((rows, voc), jnp.bfloat16),
            pltpu.SemaphoreType.DMA((4,)),
        ],
        input_output_aliases={} if filled is None else {count + 2: 0},
        compiler_params=pltpu.CompilerParams(vmem_limit_bytes=8 * 1024 * 1024),
        cost_estimate=pl.CostEstimate(
            flops=2 * rows * width * voc, bytes_accessed=2 * width * (voc + rows), transcendentals=0
        ),
    )(*operands)


def merge(stats):
    stats = jnp.stack(stats)
    own_max = jnp.max(stats[:, 0], axis=0)
    peer_max = jnp.max(stats[:, 2], axis=0)
    own_scale = jnp.exp(stats[:, 0] - own_max)
    peer_scale = jnp.exp(stats[:, 2] - peer_max)
    (terms,) = tied(
        jnp.stack([stats[:, 1] * own_scale, stats[:, 3] * peer_scale, stats[:, 4], stats[:, 5] * peer_scale])
    )
    own_sum, peer_sum, target, cross = (terms[:, 0] + terms[:, 1]) + (terms[:, 2] + terms[:, 3])
    return jnp.stack([own_max, own_sum, peer_max, peer_sum, target, cross])


def wide(block):
    return block.astype(jnp.float32)


def narrow(block):
    return block.astype(jnp.bfloat16)


def sum_rows(grad_logits, matrix, later):
    voc = grad_logits.shape[1]
    width = matrix.shape[0] // 4
    at_x, at_z = bits(lax.axis_index("tx")), bits(lax.axis_index("tz"))
    rows = grad_logits.reshape(4, 4, 4, 8, voc)
    for axis in (1, 2):
        rows = jnp.concatenate([lax.slice_in_dim(rows, j, j + 1, axis=axis) for j in (0, 3, 1, 2)], axis=axis)
    rows = rows.reshape(4, 2, 2, 2, 2, 8, voc)
    dims = {"xa": (1, at_x[0], "tx", 1), "xb": (2, at_x[1], "tx", 3), "za": (3, at_z[0], "tz", 1), "zb": (4, at_z[1], "tz", 3)}
    orders = [("xa", "xb", "za", "zb"), ("xb", "xa", "zb", "za"), ("za", "zb", "xa", "xb"), ("zb", "za", "xb", "xa")]

    def product(block, q):
        columns = matrix[q * width : (q + 1) * width]
        out = lax.dot_general(
            block.reshape(-1, voc), columns, (((1,), (1,)), ((), ())), preferred_element_type=jnp.float32
        )
        return out.reshape(block.shape[:-1] + (width,))

    def split(block, name):
        at = dims[name][1]
        away = lax.dynamic_index_in_dim(block, 1 - at, 0, keepdims=False)
        return away, lax.dynamic_index_in_dim(block, at, 0, keepdims=False)

    def swap(block, name):
        axis, step = dims[name][2:]
        return lax.ppermute(block, axis, [(i, i ^ step) for i in range(4)])

    sent, stay = [], []
    for q, order in enumerate(orders):
        turned_rows = jnp.transpose(rows, [dims[name][0] for name in order] + [0, 5, 6])
        one, other = split(turned_rows, order[0])
        sent.append(product(*tied(one), q))
        stay.append(split(other, order[1]))
    came = [swap(narrow(sent[q]), orders[q][0]) for q in range(4)]
    came[0], later = tied(came[0], later)
    kept = []
    for q, order in enumerate(orders):
        one, other = [product(part, q) + wide(block) for part, block in zip(stay[q], split(came[q], order[1]))]
        came[q] = swap(narrow(one), order[1])
        kept.append(other)
    for stage in range(2, 4):
        halves = [
            [k + wide(c) for k, c in zip(split(kept[q], orders[q][stage]), split(came[q], orders[q][stage]))]
            for q in range(4)
        ]
        came = [swap(narrow(halves[q][0]), orders[q][stage]) for q in range(4)]
        kept = [halves[q][1] for q in range(4)]
    state = [kept[q] + wide(came[q]) for q in range(4)]
    block = jnp.concatenate(state, axis=-1)
    first, second = by_core(block[NEAR], block[WRAP]), by_core(block[WRAP], block[NEAR])
    came = swap_y(narrow(jnp.stack([first, block[FAR]])), (1, 3))
    mine, rest = block[OWN] + wide(came[0]), second + wide(came[1])
    return [mine + wide(swap_y(narrow(rest), (3, 1)))], later


def shard_stats(logits, peer_logits, hit):
    values = wide(logits)
    own_max = jnp.max(jnp.maximum(values, LOWEST), axis=-1)
    own_sum = jnp.sum(jnp.exp(values - own_max[:, None]), axis=-1)
    target = jnp.sum(jnp.where(hit, values, 0.0), axis=-1)
    own_max, own_sum, target, peer_logits = tied(own_max, own_sum, target, peer_logits)
    peer_values = wide(peer_logits)
    peer_max = jnp.max(jnp.maximum(peer_values, LOWEST), axis=-1)
    peer_exp = jnp.exp(peer_values - peer_max[:, None])
    peer_sum = jnp.sum(peer_exp, axis=-1)
    cross = jnp.sum(peer_exp * (peer_values - values), axis=-1)
    row = lax.broadcasted_iota(jnp.int32, (6, own_max.shape[0]), 0)
    stats = jnp.zeros(row.shape, jnp.float32)
    for k, part in enumerate((own_max, own_sum, peer_max, peer_sum, target, cross)):
        stats = jnp.where(row == k, part[None], stats)
    return stats, peer_logits


def norm_backward_kernel(count, *refs):
    states_ref, gain_ref, out_ref = refs[count:]
    states = states_ref[...]
    width = states.shape[1]
    inverse = lax.rsqrt(jnp.sum(states * states, axis=-1, keepdims=True) / width + eps_norm)
    pieces, start = [], 0
    for ref in refs[:count]:
        columns = slice(start, start + ref.shape[1])
        pieces.append((ref[...] * gain_ref[:, columns], columns))
        start += ref.shape[1]
    inner = sum(jnp.sum(scaled * states[:, columns], axis=-1, keepdims=True) for scaled, columns in pieces) / width
    for scaled, columns in pieces:
        rows = narrow(inverse * (scaled - states[:, columns] * inverse * inverse * inner))
        for k in range(out_ref.shape[0]):
            out_ref[k, :, columns] = rows


def mean_loss(stats, weights):
    own_log = stats[0] + jnp.log(stats[1])
    peer_log = stats[2] + jnp.log(stats[3])
    per_token = own_log - stats[4] + kl_weight * (stats[5] / stats[3] - peer_log + own_log)
    sums = jnp.sum((weights * per_token).reshape(4, -1), axis=-1)
    total = (sums[OWN] + sums[NEAR]) + (sums[FAR] + sums[WRAP])
    return (total / jnp.sum(weights)).reshape((1,))


def local(hidden, gain, head, targets, lengths):
    block = hidden[0]
    gain_row = gain[0][None, :]
    matrix = head[0]
    group = block.shape[0]
    tokens = 4 * group
    voc_shard = matrix.shape[1]
    logits, ints = gather_logits(block, gain_row, matrix, jnp.concatenate([targets, lengths]))
    all_targets = jnp.concatenate([part[:group] for part in ints])
    all_lengths = jnp.concatenate([part[group:] for part in ints])
    peer_logits = lax.ppermute(logits, "peer", [(0, 1), (1, 0)])
    hit = all_targets[:, None] - lax.axis_index(("dp", "tx", "tz")) * voc_shard
    hit = hit == lax.broadcasted_iota(jnp.int32, (1, voc_shard), 1)
    stats, peer_logits = shard_stats(logits, peer_logits, hit)
    stats = merge(ring(stats, "tz"))
    stats = merge(ring(stats, "tx"))
    stats = merge(ring(stats, "dp", lambda block, step: turned(block, step, 1)))
    own_log = stats[0] + jnp.log(stats[1])
    peer_log = stats[2] + jnp.log(stats[3])
    values, peer_values = wide(logits), wide(peer_logits)
    sequence = lax.broadcasted_iota(jnp.int32, (all_lengths.shape[0], tokens), 0)
    token = lax.broadcasted_iota(jnp.int32, sequence.shape, 1)
    limits = jnp.sum(jnp.where(token // LEN == sequence, all_lengths[:, None], 0), axis=0)
    weights = (lax.broadcasted_iota(jnp.int32, (tokens,), 0) % LEN < limits).astype(jnp.float32)

    grad_logits = (
        loss_scale
        * weights[:, None]
        * (
            (1.0 + kl_weight) * jnp.exp(values - own_log[:, None])
            - hit.astype(jnp.float32)
            - kl_weight * jnp.exp(peer_values - peer_log[:, None])
        )
    ).astype(jnp.bfloat16)
    grad_normed, stats = sum_rows(grad_logits, matrix, stats)
    loss = mean_loss(stats, weights)

    own = lax.dynamic_slice_in_dim(block, lax.axis_index(("tx", "tz")) * 8, 8, axis=0)
    spread = pl.pallas_call(
        functools.partial(norm_backward_kernel, len(grad_normed)),
        out_shape=jax.ShapeDtypeStruct((16,) + own.shape, own.dtype),
        compiler_params=pltpu.CompilerParams(vmem_limit_bytes=16 * 1024 * 1024),
    )(*grad_normed, wide(own), gain_row)
    grad_hidden = lax.all_to_all(spread, ("tx", "tz"), split_axis=0, concat_axis=0, tiled=True)
    return (loss, grad_hidden.reshape((1,) + block.shape))


def solution(mesh):
    cube = Mesh(mesh.devices.reshape(2, 4, 4, 4), ALL)
    return jax.shard_map(
        local,
        mesh=cube,
        in_specs=(
            P("peer", "dp", None),
            P("peer", None),
            P("peer", None, ("dp", "tx", "tz")),
            P("dp"),
            P("dp"),
        ),
        out_specs=(P("peer"), P("peer", "dp", None)),
        check_vma=False,
    )
```

```python
import functools

import jax
import jax.numpy as jnp
from jax import lax
from jax.experimental import pallas as pl
from jax.experimental.pallas import tpu as pltpu
from jax.sharding import Mesh, PartitionSpec as P

LEN = 32
TILE = 128

kl_weight = 0.5
loss_scale = 64.0
eps_norm = 1e-06

LOWEST = -3.4e38

ALL = ("peer", "dp", "tx", "tz")

OWN, NEAR, WRAP, FAR = range(4)
FLIP = {1: 1, 2: 3, 3: 2}


def permute(block, move):
    def index(core, y, x, z):
        return ((core * 4 + y) * 4 + x) * 4 + z

    places = [(c, y, x, z) for c in range(2) for y in range(4) for x in range(4) for z in range(4)]
    return lax.ppermute(block, ALL, [(index(*p), index(*move(*p))) for p in places])


def swap_u(block, step):
    return permute(block, lambda c, y, x, z: (c, y, x ^ step, z) if c == 0 else (c, y, x, z ^ step))


def swap_y(block, steps):
    return permute(block, lambda c, y, x, z: (c, y ^ steps[c], x, z))


def core():
    return lax.axis_index("peer")


def by_core(first, second):
    return jnp.where(core() == 0, first, second)


def bits(position):
    return (position ^ (position >> 1)) & 1, position >> 1


def parity():
    return (lax.axis_index("tx") + lax.axis_index("tz")) & 1


def tied(*blocks):
    return lax.optimization_barrier(blocks)


def ring(block, axis, prepare=lambda block, step: block):
    far, near, wrap = [
        lax.ppermute(prepare(block, step), axis, [(i, i ^ step) for i in range(4)]) for step in (2, 1, 3)
    ]
    return [block, near, far, wrap]


def turned(block, step, axis):
    size = block.shape[axis] // 4
    parts = [lax.slice_in_dim(block, p * size, (p + 1) * size, axis=axis) for p in range(4)]
    return jnp.concatenate([parts[p ^ FLIP[step]] for p in range(4)], axis=axis)


def gather_logits(block, gain_row, matrix, ints):
    half = block.shape[0] // 2
    tokens = 4 * block.shape[0]
    mine = lax.dynamic_slice_in_dim(block, parity() * half, half, axis=0)
    p = swap_y(mine, (1, 3))
    q = swap_y(mine, (3, 1))
    ints = ring(ints, "dp")
    logits, matrix = add_logits((block,), OWN_PLAN, gain_row, matrix, tokens)
    p, q, logits, *ints = tied(p, q, logits, *ints)
    far = swap_y(q, (1, 3))
    p_side, q_side = swap_u(p, 1), swap_u(q, 3)
    logits, matrix = add_logits((p, q), HELD_PLAN, gain_row, matrix, tokens, logits)
    far, logits = tied(far, logits)
    far_sides = [swap_u(far[: half // 2], 1), swap_u(far[half // 2 :], 3)]
    logits, matrix = add_logits((p_side, q_side), OTHER_PLAN, gain_row, matrix, tokens, logits)
    logits, matrix = add_logits((far, *far_sides), FAR_PLAN, gain_row, matrix, tokens, logits)
    return logits, matrix, [ints[s] for s in (0, 1, 3, 2)]


def make_kernel(count, streamed, loads, stores):
    def kernel(*refs):
        sources = refs[:count]
        gain_ref, head_ref = refs[count : count + 2]
        out_ref, held_head, rows, sums, total, block, sems, head_sems = refs[-8:]
        width = rows.shape[1]
        held = parity() * 64
        p_first = 128 * (NEAR + core() * (WRAP - NEAR))
        q_first = 128 * (NEAR + WRAP) - p_first
        shift = {"all": 0, "held": held, "other": 64 - held}
        shift |= {"p held": p_first + held, "q held": q_first + held}
        shift |= {"p other": p_first + 64 - held, "q other": q_first + 64 - held}
        copies = []
        for source, start, length, target, kind in loads:
            to = pl.multiple_of(shift[kind] + target, 16)
            copies.append(
                pltpu.make_async_copy(
                    sources[source].at[pl.ds(start, length)], rows.at[pl.ds(to, length)], sems.at[len(copies)]
                )
            )
        depth = 1024
        fetches = []
        if streamed:
            for c in range(0, width, depth // 2):
                piece = pl.ds(c, depth // 2)
                fetches.append(
                    pltpu.make_async_copy(head_ref.at[piece], held_head.at[piece], head_sems.at[len(fetches)])
                )
        for copy in copies + fetches:
            copy.start()
        for copy in copies:
            copy.wait()

        @pl.loop(0, rows.shape[0] // 16)
        def _(step):
            piece = pl.ds(pl.multiple_of(step * 16, 16), 16)
            lanes = jnp.zeros((16, TILE), jnp.float32)
            for c in range(0, width, TILE):
                states = rows[piece, c : c + TILE].astype(jnp.float32)
                lanes += states * states
            sums[piece, :] = lanes

        mean = jnp.sum(sums[...], axis=-1, keepdims=True) / width
        sums[...] = jnp.broadcast_to(lax.rsqrt(mean + eps_norm), sums.shape)

        @pl.loop(0, rows.shape[0] // 16)
        def _(step):
            piece = pl.ds(pl.multiple_of(step * 16, 16), 16)
            inverse = sums[piece, :]
            for c in range(0, width, TILE):
                states = rows[piece, c : c + TILE].astype(jnp.float32)
                rows[piece, c : c + TILE] = (states * inverse * gain_ref[:, c : c + TILE]).astype(jnp.bfloat16)

        for c in range(0, width, depth):
            for copy in fetches[2 * c // depth : 2 * c // depth + 2]:
                copy.wait()
            part = jnp.dot(rows[:, c : c + depth], held_head[c : c + depth, :], preferred_element_type=jnp.float32)
            if c == 0:
                total[...] = part
            elif c + depth < width:
                total[...] += part
            else:
                block[...] = (total[...] + part).astype(jnp.bfloat16)
        copies = []
        for start, length, target, kind in stores:
            to = pl.multiple_of(shift[kind] + target, 16)
            copies.append(
                pltpu.make_async_copy(
                    block.at[pl.ds(start, length)], out_ref.at[pl.ds(to, length)], sems.at[len(copies)]
                )
            )
        for copy in copies:
            copy.start()
        for copy in copies:
            copy.wait()

    return kernel


OWN_PLAN = [(0, 0, 128, 0, "all")], [(0, 128, 0, "all")]
HELD_PLAN = [(0, 0, 64, 0, "all"), (1, 0, 64, 64, "all")], [(0, 64, 0, "p held"), (64, 64, 0, "q held")]
OTHER_PLAN = [(0, 0, 64, 0, "all"), (1, 0, 64, 64, "all")], [(0, 64, 0, "p other"), (64, 64, 0, "q other")]
FAR_PLAN = (
    [(0, 0, 64, 0, "held")] + [(1 + k, 0, 32, 32 * k, "other") for k in range(2)],
    [(0, 128, FAR * 128, "all")],
)


def add_logits(sources, plan, gain_row, matrix, tokens, filled=None):
    width, voc = matrix.shape
    anywhere = pl.BlockSpec(memory_space=pl.ANY)
    count = len(sources)
    rows = sum(piece[2] for piece in plan[0])
    streamed = filled is None
    operands = [*sources, gain_row, matrix] + ([] if filled is None else [filled])
    return pl.pallas_call(
        make_kernel(count, streamed, *plan),
        out_shape=(
            jax.ShapeDtypeStruct((tokens, voc), jnp.bfloat16),
            jax.ShapeDtypeStruct(matrix.shape, matrix.dtype),
        ),
        in_specs=[anywhere] * count
        + [pl.BlockSpec(memory_space=pltpu.VMEM), anywhere if streamed else pl.BlockSpec(memory_space=pltpu.VMEM)]
        + ([] if filled is None else [anywhere]),
        out_specs=(anywhere, pl.BlockSpec(memory_space=pltpu.VMEM)),
        scratch_shapes=[
            pltpu.VMEM((rows, width), jnp.bfloat16),
            pltpu.VMEM((rows, TILE), jnp.float32),
            pltpu.VMEM((rows, voc), jnp.float32),
            pltpu.VMEM((rows, voc), jnp.bfloat16),
            pltpu.SemaphoreType.DMA((4,)),
            pltpu.SemaphoreType.DMA((10,)),
        ],
        input_output_aliases={} if streamed else {count + 1: 1, count + 2: 0},
        compiler_params=pltpu.CompilerParams(vmem_limit_bytes=8 * 1024 * 1024),
        cost_estimate=pl.CostEstimate(
            flops=2 * rows * width * voc, bytes_accessed=2 * width * (voc + rows), transcendentals=0
        ),
    )(*operands)


def merge(stats):
    stats = jnp.stack(stats)
    own_max = jnp.max(stats[:, 0], axis=0)
    peer_max = jnp.max(stats[:, 2], axis=0)
    own_scale = jnp.exp(stats[:, 0] - own_max)
    peer_scale = jnp.exp(stats[:, 2] - peer_max)
    (terms,) = tied(
        jnp.stack([stats[:, 1] * own_scale, stats[:, 3] * peer_scale, stats[:, 4], stats[:, 5] * peer_scale])
    )
    own_sum, peer_sum, target, cross = (terms[:, 0] + terms[:, 1]) + (terms[:, 2] + terms[:, 3])
    return jnp.stack([own_max, own_sum, peer_max, peer_sum, target, cross])


def wide(block):
    return block.astype(jnp.float32)


def narrow(block):
    return block.astype(jnp.bfloat16)


def sum_rows(grad_logits, matrix, later):
    voc = grad_logits.shape[1]
    width = matrix.shape[0] // 4
    at_x, at_z = bits(lax.axis_index("tx")), bits(lax.axis_index("tz"))
    rows = grad_logits.reshape(4, 4, 4, 8, voc)
    for axis in (1, 2):
        rows = jnp.concatenate([lax.slice_in_dim(rows, j, j + 1, axis=axis) for j in (0, 3, 1, 2)], axis=axis)
    rows = rows.reshape(4, 2, 2, 2, 2, 8, voc)
    dims = {"xa": (1, at_x[0], "tx", 1), "xb": (2, at_x[1], "tx", 3), "za": (3, at_z[0], "tz", 1), "zb": (4, at_z[1], "tz", 3)}
    orders = [("xa", "xb", "za", "zb"), ("xb", "xa", "zb", "za"), ("za", "zb", "xa", "xb"), ("zb", "za", "xb", "xa")]

    def product(block, q):
        columns = matrix[q * width : (q + 1) * width]
        out = lax.dot_general(
            block.reshape(-1, voc), columns, (((1,), (1,)), ((), ())), preferred_element_type=jnp.float32
        )
        return out.reshape(block.shape[:-1] + (width,))

    def split(block, name):
        at = dims[name][1]
        away = lax.dynamic_index_in_dim(block, 1 - at, 0, keepdims=False)
        return away, lax.dynamic_index_in_dim(block, at, 0, keepdims=False)

    def swap(block, name):
        axis, step = dims[name][2:]
        return lax.ppermute(block, axis, [(i, i ^ step) for i in range(4)])

    sent, stay = [], []
    for q, order in enumerate(orders):
        turned_rows = jnp.transpose(rows, [dims[name][0] for name in order] + [0, 5, 6])
        one, other = split(turned_rows, order[0])
        sent.append(product(*tied(one), q))
        stay.append(split(other, order[1]))
    came = [swap(narrow(sent[q]), orders[q][0]) for q in range(4)]
    came[0], later = tied(came[0], later)
    kept = []
    for q, order in enumerate(orders):
        one, other = [product(part, q) + wide(block) for part, block in zip(stay[q], split(came[q], order[1]))]
        came[q] = swap(narrow(one), order[1])
        kept.append(other)
    for stage in range(2, 4):
        halves = [
            [k + wide(c) for k, c in zip(split(kept[q], orders[q][stage]), split(came[q], orders[q][stage]))]
            for q in range(4)
        ]
        came = [swap(narrow(halves[q][0]), orders[q][stage]) for q in range(4)]
        kept = [halves[q][1] for q in range(4)]
    state = [kept[q] + wide(came[q]) for q in range(4)]
    block = jnp.concatenate(state, axis=-1)
    first, second = by_core(block[NEAR], block[WRAP]), by_core(block[WRAP], block[NEAR])
    came = swap_y(narrow(jnp.stack([first, block[FAR]])), (1, 3))
    mine, rest = block[OWN] + wide(came[0]), second + wide(came[1])
    return [mine + wide(swap_y(narrow(rest), (3, 1)))], later


def shard_stats(logits, peer_logits, hit):
    values = wide(logits)
    own_max = jnp.max(jnp.maximum(values, LOWEST), axis=-1)
    own_sum = jnp.sum(jnp.exp(values - own_max[:, None]), axis=-1)
    target = jnp.sum(jnp.where(hit, values, 0.0), axis=-1)
    own_max, own_sum, target, peer_logits = tied(own_max, own_sum, target, peer_logits)
    peer_values = wide(peer_logits)
    peer_max = jnp.max(jnp.maximum(peer_values, LOWEST), axis=-1)
    peer_exp = jnp.exp(peer_values - peer_max[:, None])
    peer_sum = jnp.sum(peer_exp, axis=-1)
    cross = jnp.sum(peer_exp * (peer_values - values), axis=-1)
    row = lax.broadcasted_iota(jnp.int32, (6, own_max.shape[0]), 0)
    stats = jnp.zeros(row.shape, jnp.float32)
    for k, part in enumerate((own_max, own_sum, peer_max, peer_sum, target, cross)):
        stats = jnp.where(row == k, part[None], stats)
    return stats, peer_logits


def norm_backward_kernel(count, *refs):
    states_ref, gain_ref, out_ref = refs[count:]
    states = states_ref[...]
    width = states.shape[1]
    inverse = lax.rsqrt(jnp.sum(states * states, axis=-1, keepdims=True) / width + eps_norm)
    pieces, start = [], 0
    for ref in refs[:count]:
        columns = slice(start, start + ref.shape[1])
        pieces.append((ref[...] * gain_ref[:, columns], columns))
        start += ref.shape[1]
    inner = sum(jnp.sum(scaled * states[:, columns], axis=-1, keepdims=True) for scaled, columns in pieces) / width
    for scaled, columns in pieces:
        rows = narrow(inverse * (scaled - states[:, columns] * inverse * inverse * inner))
        for k in range(out_ref.shape[0]):
            out_ref[k, :, columns] = rows


def mean_loss(per_token, weights):
    sums = jnp.sum(per_token.reshape(4, -1), axis=-1)
    total = (sums[OWN] + sums[NEAR]) + (sums[FAR] + sums[WRAP])
    return (total / jnp.sum(weights)).reshape((1,))


def local(hidden, gain, head, targets, lengths):
    block = hidden[0]
    gain_row = gain[0][None, :]
    matrix = head[0]
    group = block.shape[0]
    tokens = 4 * group
    voc_shard = matrix.shape[1]
    logits, matrix, ints = gather_logits(block, gain_row, matrix, jnp.concatenate([targets, lengths]))
    all_targets = jnp.concatenate([part[:group] for part in ints])
    all_lengths = jnp.concatenate([part[group:] for part in ints])
    peer_logits = lax.ppermute(logits, "peer", [(0, 1), (1, 0)])
    hit = all_targets[:, None] - lax.axis_index(("dp", "tx", "tz")) * voc_shard
    hit = hit == lax.broadcasted_iota(jnp.int32, (1, voc_shard), 1)
    stats, peer_logits = shard_stats(logits, peer_logits, hit)
    stats = merge(ring(stats, "tz"))
    stats = merge(ring(stats, "tx"))
    stats = merge(ring(stats, "dp", lambda block, step: turned(block, step, 1)))
    own_log = stats[0] + jnp.log(stats[1])
    peer_log = stats[2] + jnp.log(stats[3])
    values, peer_values = wide(logits), wide(peer_logits)
    sequence = lax.broadcasted_iota(jnp.int32, (all_lengths.shape[0], tokens), 0)
    token = lax.broadcasted_iota(jnp.int32, sequence.shape, 1)
    limits = jnp.sum(jnp.where(token // LEN == sequence, all_lengths[:, None], 0), axis=0)
    weights = (lax.broadcasted_iota(jnp.int32, (tokens,), 0) % LEN < limits).astype(jnp.float32)

    grad_logits = (
        loss_scale
        * weights[:, None]
        * (
            (1.0 + kl_weight) * jnp.exp(values - own_log[:, None])
            - hit.astype(jnp.float32)
            - kl_weight * jnp.exp(peer_values - peer_log[:, None])
        )
    ).astype(jnp.bfloat16)
    per_token = own_log - stats[4] + kl_weight * (stats[5] / stats[3] - peer_log + own_log)
    grad_normed, per_token = sum_rows(grad_logits, matrix, weights * per_token)
    loss = mean_loss(per_token, weights)

    own = lax.dynamic_slice_in_dim(block, lax.axis_index(("tx", "tz")) * 8, 8, axis=0)
    spread = pl.pallas_call(
        functools.partial(norm_backward_kernel, len(grad_normed)),
        out_shape=jax.ShapeDtypeStruct((16,) + own.shape, own.dtype),
        compiler_params=pltpu.CompilerParams(vmem_limit_bytes=16 * 1024 * 1024),
    )(*grad_normed, wide(own), gain_row)
    grad_hidden = lax.all_to_all(spread, ("tx", "tz"), split_axis=0, concat_axis=0, tiled=True)
    return (loss, grad_hidden.reshape((1,) + block.shape))


def solution(mesh):
    cube = Mesh(mesh.devices.reshape(2, 4, 4, 4), ALL)
    return jax.shard_map(
        local,
        mesh=cube,
        in_specs=(
            P("peer", "dp", None),
            P("peer", None),
            P("peer", None, ("dp", "tx", "tz")),
            P("dp"),
            P("dp"),
        ),
        out_specs=(P("peer"), P("peer", "dp", None)),
        check_vma=False,
    )
```

```python
import functools

import jax
import jax.numpy as jnp
from jax import lax
from jax.experimental import pallas as pl
from jax.experimental.pallas import tpu as pltpu
from jax.sharding import Mesh, PartitionSpec as P

LEN = 32
TILE = 128

kl_weight = 0.5
loss_scale = 64.0
eps_norm = 1e-06

LOWEST = -3.4e38

ALL = ("peer", "dp", "tx", "tz")

OWN, NEAR, WRAP, FAR = range(4)
FLIP = {1: 1, 2: 3, 3: 2}


def permute(block, move):
    def index(core, y, x, z):
        return ((core * 4 + y) * 4 + x) * 4 + z

    places = [(c, y, x, z) for c in range(2) for y in range(4) for x in range(4) for z in range(4)]
    return lax.ppermute(block, ALL, [(index(*p), index(*move(*p))) for p in places])


def swap_u(block, step):
    return permute(block, lambda c, y, x, z: (c, y, x ^ step, z) if c == 0 else (c, y, x, z ^ step))


def swap_y(block, steps):
    return permute(block, lambda c, y, x, z: (c, y ^ steps[c], x, z))


def core():
    return lax.axis_index("peer")


def by_core(first, second):
    return jnp.where(core() == 0, first, second)


def bits(position):
    return (position ^ (position >> 1)) & 1, position >> 1


def parity():
    return (lax.axis_index("tx") + lax.axis_index("tz")) & 1


def tied(*blocks):
    return lax.optimization_barrier(blocks)


def ring(block, axis, prepare=lambda block, step: block):
    far, near, wrap = [
        lax.ppermute(prepare(block, step), axis, [(i, i ^ step) for i in range(4)]) for step in (2, 1, 3)
    ]
    return [block, near, far, wrap]


def turned(block, step, axis):
    size = block.shape[axis] // 4
    parts = [lax.slice_in_dim(block, p * size, (p + 1) * size, axis=axis) for p in range(4)]
    return jnp.concatenate([parts[p ^ FLIP[step]] for p in range(4)], axis=axis)


def gather_logits(block, gain_row, matrix, ints):
    half = block.shape[0] // 2
    tokens = 4 * block.shape[0]
    mine = lax.dynamic_slice_in_dim(block, parity() * half, half, axis=0)
    p = swap_y(mine, (1, 3))
    q = swap_y(mine, (3, 1))
    ints = ring(ints, "dp")
    logits, matrix = add_logits((block,), OWN_PLAN, gain_row, matrix, tokens)
    p, q, logits, *ints = tied(p, q, logits, *ints)
    far = swap_y(q, (1, 3))
    p_side, q_side = swap_u(p, 1), swap_u(q, 3)
    logits, matrix = add_logits((p, q), HELD_PLAN, gain_row, matrix, tokens, logits)
    far, logits = tied(far, logits)
    far_sides = [swap_u(far[: half // 2], 1), swap_u(far[half // 2 :], 3)]
    logits, matrix = add_logits((p_side, q_side), OTHER_PLAN, gain_row, matrix, tokens, logits)
    logits, _ = add_logits((far, *far_sides), FAR_PLAN, gain_row, matrix, tokens, logits)
    return logits, [ints[s] for s in (0, 1, 3, 2)]


def make_kernel(count, streamed, loads, stores):
    def kernel(*refs):
        sources = refs[:count]
        gain_ref, head_ref = refs[count : count + 2]
        out_ref, held_head, rows, sums, total, block, sems, head_sems = refs[-8:]
        width = rows.shape[1]
        held = parity() * 64
        p_first = 128 * (NEAR + core() * (WRAP - NEAR))
        q_first = 128 * (NEAR + WRAP) - p_first
        shift = {"all": 0, "held": held, "other": 64 - held}
        shift |= {"p held": p_first + held, "q held": q_first + held}
        shift |= {"p other": p_first + 64 - held, "q other": q_first + 64 - held}
        copies = []
        for source, start, length, target, kind in loads:
            to = pl.multiple_of(shift[kind] + target, 16)
            copies.append(
                pltpu.make_async_copy(
                    sources[source].at[pl.ds(start, length)], rows.at[pl.ds(to, length)], sems.at[len(copies)]
                )
            )
        depth = 1024
        fetches = []
        if streamed:
            for c in range(0, width, depth // 2):
                piece = pl.ds(c, depth // 2)
                fetches.append(
                    pltpu.make_async_copy(head_ref.at[piece], held_head.at[piece], head_sems.at[len(fetches)])
                )
        for copy in copies + fetches:
            copy.start()
        for copy in copies:
            copy.wait()

        @pl.loop(0, rows.shape[0] // 16)
        def _(step):
            piece = pl.ds(pl.multiple_of(step * 16, 16), 16)
            lanes = jnp.zeros((16, TILE), jnp.float32)
            for c in range(0, width, TILE):
                states = rows[piece, c : c + TILE].astype(jnp.float32)
                lanes += states * states
            sums[piece, :] = lanes

        mean = jnp.sum(sums[...], axis=-1, keepdims=True) / width
        sums[...] = jnp.broadcast_to(lax.rsqrt(mean + eps_norm), sums.shape)

        @pl.loop(0, rows.shape[0] // 16)
        def _(step):
            piece = pl.ds(pl.multiple_of(step * 16, 16), 16)
            inverse = sums[piece, :]
            for c in range(0, width, TILE):
                states = rows[piece, c : c + TILE].astype(jnp.float32)
                rows[piece, c : c + TILE] = (states * inverse * gain_ref[:, c : c + TILE]).astype(jnp.bfloat16)

        for c in range(0, width, depth):
            for copy in fetches[2 * c // depth : 2 * c // depth + 2]:
                copy.wait()
            part = jnp.dot(rows[:, c : c + depth], held_head[c : c + depth, :], preferred_element_type=jnp.float32)
            if c == 0:
                total[...] = part
            elif c + depth < width:
                total[...] += part
            else:
                block[...] = (total[...] + part).astype(jnp.bfloat16)
        copies = []
        for start, length, target, kind in stores:
            to = pl.multiple_of(shift[kind] + target, 16)
            copies.append(
                pltpu.make_async_copy(
                    block.at[pl.ds(start, length)], out_ref.at[pl.ds(to, length)], sems.at[len(copies)]
                )
            )
        for copy in copies:
            copy.start()
        for copy in copies:
            copy.wait()

    return kernel


OWN_PLAN = [(0, 0, 128, 0, "all")], [(0, 128, 0, "all")]
HELD_PLAN = [(0, 0, 64, 0, "all"), (1, 0, 64, 64, "all")], [(0, 64, 0, "p held"), (64, 64, 0, "q held")]
OTHER_PLAN = [(0, 0, 64, 0, "all"), (1, 0, 64, 64, "all")], [(0, 64, 0, "p other"), (64, 64, 0, "q other")]
FAR_PLAN = (
    [(0, 0, 64, 0, "held")] + [(1 + k, 0, 32, 32 * k, "other") for k in range(2)],
    [(0, 128, FAR * 128, "all")],
)


def add_logits(sources, plan, gain_row, matrix, tokens, filled=None):
    width, voc = matrix.shape
    anywhere = pl.BlockSpec(memory_space=pl.ANY)
    count = len(sources)
    rows = sum(piece[2] for piece in plan[0])
    streamed = filled is None
    operands = [*sources, gain_row, matrix] + ([] if filled is None else [filled])
    return pl.pallas_call(
        make_kernel(count, streamed, *plan),
        out_shape=(
            jax.ShapeDtypeStruct((tokens, voc), jnp.bfloat16),
            jax.ShapeDtypeStruct(matrix.shape, matrix.dtype),
        ),
        in_specs=[anywhere] * count
        + [pl.BlockSpec(memory_space=pltpu.VMEM), anywhere if streamed else pl.BlockSpec(memory_space=pltpu.VMEM)]
        + ([] if filled is None else [anywhere]),
        out_specs=(anywhere, pl.BlockSpec(memory_space=pltpu.VMEM)),
        scratch_shapes=[
            pltpu.VMEM((rows, width), jnp.bfloat16),
            pltpu.VMEM((rows, TILE), jnp.float32),
            pltpu.VMEM((rows, voc), jnp.float32),
            pltpu.VMEM((rows, voc), jnp.bfloat16),
            pltpu.SemaphoreType.DMA((4,)),
            pltpu.SemaphoreType.DMA((10,)),
        ],
        input_output_aliases={} if streamed else {count + 1: 1, count + 2: 0},
        compiler_params=pltpu.CompilerParams(vmem_limit_bytes=8 * 1024 * 1024),
        cost_estimate=pl.CostEstimate(
            flops=2 * rows * width * voc, bytes_accessed=2 * width * (voc + rows), transcendentals=0
        ),
    )(*operands)


def merge(stats):
    stats = jnp.stack(stats)
    own_max = jnp.max(stats[:, 0], axis=0)
    peer_max = jnp.max(stats[:, 2], axis=0)
    own_scale = jnp.exp(stats[:, 0] - own_max)
    peer_scale = jnp.exp(stats[:, 2] - peer_max)
    (terms,) = tied(
        jnp.stack([stats[:, 1] * own_scale, stats[:, 3] * peer_scale, stats[:, 4], stats[:, 5] * peer_scale])
    )
    own_sum, peer_sum, target, cross = (terms[:, 0] + terms[:, 1]) + (terms[:, 2] + terms[:, 3])
    return jnp.stack([own_max, own_sum, peer_max, peer_sum, target, cross])


def wide(block):
    return block.astype(jnp.float32)


def narrow(block):
    return block.astype(jnp.bfloat16)


def sum_rows(grad_logits, matrix, later):
    voc = grad_logits.shape[1]
    width = matrix.shape[0] // 4
    at_x, at_z = bits(lax.axis_index("tx")), bits(lax.axis_index("tz"))
    rows = grad_logits.reshape(4, 4, 4, 8, voc)
    for axis in (1, 2):
        rows = jnp.concatenate([lax.slice_in_dim(rows, j, j + 1, axis=axis) for j in (0, 3, 1, 2)], axis=axis)
    rows = rows.reshape(4, 2, 2, 2, 2, 8, voc)
    dims = {"xa": (1, at_x[0], "tx", 1), "xb": (2, at_x[1], "tx", 3), "za": (3, at_z[0], "tz", 1), "zb": (4, at_z[1], "tz", 3)}
    orders = [("xa", "xb", "za", "zb"), ("xb", "xa", "zb", "za"), ("za", "zb", "xa", "xb"), ("zb", "za", "xb", "xa")]

    def product(block, q):
        columns = matrix[q * width : (q + 1) * width]
        out = lax.dot_general(
            block.reshape(-1, voc), columns, (((1,), (1,)), ((), ())), preferred_element_type=jnp.float32
        )
        return out.reshape(block.shape[:-1] + (width,))

    def split(block, name):
        at = dims[name][1]
        away = lax.dynamic_index_in_dim(block, 1 - at, 0, keepdims=False)
        return away, lax.dynamic_index_in_dim(block, at, 0, keepdims=False)

    def swap(block, name):
        axis, step = dims[name][2:]
        return lax.ppermute(block, axis, [(i, i ^ step) for i in range(4)])

    sent, stay = [], []
    for q, order in enumerate(orders):
        turned_rows = jnp.transpose(rows, [dims[name][0] for name in order] + [0, 5, 6])
        one, other = split(turned_rows, order[0])
        sent.append(product(*tied(one), q))
        stay.append(split(other, order[1]))
    came = [swap(narrow(sent[q]), orders[q][0]) for q in range(4)]
    came[0], later = tied(came[0], later)
    kept = []
    for q, order in enumerate(orders):
        one, other = [product(part, q) + wide(block) for part, block in zip(stay[q], split(came[q], order[1]))]
        came[q] = swap(narrow(one), order[1])
        kept.append(other)
    for stage in range(2, 4):
        halves = [
            [k + wide(c) for k, c in zip(split(kept[q], orders[q][stage]), split(came[q], orders[q][stage]))]
            for q in range(4)
        ]
        came = [swap(narrow(halves[q][0]), orders[q][stage]) for q in range(4)]
        kept = [halves[q][1] for q in range(4)]
    state = [kept[q] + wide(came[q]) for q in range(4)]
    block = jnp.concatenate(state, axis=-1)
    first, second = by_core(block[NEAR], block[WRAP]), by_core(block[WRAP], block[NEAR])
    came = swap_y(narrow(jnp.stack([first, block[FAR]])), (1, 3))
    mine, rest = block[OWN] + wide(came[0]), second + wide(came[1])
    return [mine + wide(swap_y(narrow(rest), (3, 1)))], later


def shard_stats(logits, peer_logits, hit):
    values = wide(logits)
    own_max = jnp.max(jnp.maximum(values, LOWEST), axis=-1)
    own_sum = jnp.sum(jnp.exp(values - own_max[:, None]), axis=-1)
    target = jnp.sum(jnp.where(hit, values, 0.0), axis=-1)
    own_max, own_sum, target, peer_logits = tied(own_max, own_sum, target, peer_logits)
    peer_values = wide(peer_logits)
    peer_max = jnp.max(jnp.maximum(peer_values, LOWEST), axis=-1)
    peer_exp = jnp.exp(peer_values - peer_max[:, None])
    peer_sum = jnp.sum(peer_exp, axis=-1)
    cross = jnp.sum(peer_exp * (peer_values - values), axis=-1)
    row = lax.broadcasted_iota(jnp.int32, (6, own_max.shape[0]), 0)
    stats = jnp.zeros(row.shape, jnp.float32)
    for k, part in enumerate((own_max, own_sum, peer_max, peer_sum, target, cross)):
        stats = jnp.where(row == k, part[None], stats)
    return stats, peer_logits


def norm_backward_kernel(count, *refs):
    states_ref, gain_ref, out_ref = refs[count:]
    states = states_ref[...]
    width = states.shape[1]
    inverse = lax.rsqrt(jnp.sum(states * states, axis=-1, keepdims=True) / width + eps_norm)
    pieces, start = [], 0
    for ref in refs[:count]:
        columns = slice(start, start + ref.shape[1])
        pieces.append((ref[...] * gain_ref[:, columns], columns))
        start += ref.shape[1]
    inner = sum(jnp.sum(scaled * states[:, columns], axis=-1, keepdims=True) for scaled, columns in pieces) / width
    for scaled, columns in pieces:
        rows = narrow(inverse * (scaled - states[:, columns] * inverse * inverse * inner))
        for k in range(out_ref.shape[0]):
            out_ref[k, :, columns] = rows


def mean_loss(per_token, weights):
    sums = jnp.sum(per_token.reshape(4, -1), axis=-1)
    total = (sums[OWN] + sums[NEAR]) + (sums[FAR] + sums[WRAP])
    return (total / jnp.sum(weights)).reshape((1,))


def local(hidden, gain, head, targets, lengths):
    block = hidden[0]
    gain_row = gain[0][None, :]
    matrix = head[0]
    group = block.shape[0]
    tokens = 4 * group
    voc_shard = matrix.shape[1]
    logits, ints = gather_logits(block, gain_row, matrix, jnp.concatenate([targets, lengths]))
    all_targets = jnp.concatenate([part[:group] for part in ints])
    all_lengths = jnp.concatenate([part[group:] for part in ints])
    peer_logits = lax.ppermute(logits, "peer", [(0, 1), (1, 0)])
    hit = all_targets[:, None] - lax.axis_index(("dp", "tx", "tz")) * voc_shard
    hit = hit == lax.broadcasted_iota(jnp.int32, (1, voc_shard), 1)
    stats, peer_logits = shard_stats(logits, peer_logits, hit)
    stats = merge(ring(stats, "tz"))
    stats = merge(ring(stats, "tx"))
    stats = merge(ring(stats, "dp", lambda block, step: turned(block, step, 1)))
    own_log = stats[0] + jnp.log(stats[1])
    peer_log = stats[2] + jnp.log(stats[3])
    values, peer_values = wide(logits), wide(peer_logits)
    sequence = lax.broadcasted_iota(jnp.int32, (all_lengths.shape[0], tokens), 0)
    token = lax.broadcasted_iota(jnp.int32, sequence.shape, 1)
    limits = jnp.sum(jnp.where(token // LEN == sequence, all_lengths[:, None], 0), axis=0)
    weights = (lax.broadcasted_iota(jnp.int32, (tokens,), 0) % LEN < limits).astype(jnp.float32)

    grad_logits = (
        loss_scale
        * weights[:, None]
        * (
            (1.0 + kl_weight) * jnp.exp(values - own_log[:, None])
            - hit.astype(jnp.float32)
            - kl_weight * jnp.exp(peer_values - peer_log[:, None])
        )
    ).astype(jnp.bfloat16)
    per_token = own_log - stats[4] + kl_weight * (stats[5] / stats[3] - peer_log + own_log)
    grad_normed, per_token = sum_rows(grad_logits, matrix, weights * per_token)
    loss = mean_loss(per_token, weights)

    own = lax.dynamic_slice_in_dim(block, lax.axis_index(("tx", "tz")) * 8, 8, axis=0)
    spread = pl.pallas_call(
        functools.partial(norm_backward_kernel, len(grad_normed)),
        out_shape=jax.ShapeDtypeStruct((16,) + own.shape, own.dtype),
        compiler_params=pltpu.CompilerParams(vmem_limit_bytes=16 * 1024 * 1024),
    )(*grad_normed, wide(own), gain_row)
    grad_hidden = lax.all_to_all(spread, ("tx", "tz"), split_axis=0, concat_axis=0, tiled=True)
    return (loss, grad_hidden.reshape((1,) + block.shape))


def solution(mesh):
    cube = Mesh(mesh.devices.reshape(2, 4, 4, 4), ALL)
    return jax.shard_map(
        local,
        mesh=cube,
        in_specs=(
            P("peer", "dp", None),
            P("peer", None),
            P("peer", None, ("dp", "tx", "tz")),
            P("dp"),
            P("dp"),
        ),
        out_specs=(P("peer"), P("peer", "dp", None)),
        check_vma=False,
    )
```

```python
import functools

import jax
import jax.numpy as jnp
from jax import lax
from jax.experimental import pallas as pl
from jax.experimental.pallas import tpu as pltpu
from jax.sharding import Mesh, PartitionSpec as P

LEN = 32
TILE = 128

kl_weight = 0.5
loss_scale = 64.0
eps_norm = 1e-06

LOWEST = -3.4e38

ALL = ("peer", "dp", "tx", "tz")

OWN, NEAR, WRAP, FAR = range(4)
FLIP = {1: 1, 2: 3, 3: 2}


def permute(block, move):
    def index(core, y, x, z):
        return ((core * 4 + y) * 4 + x) * 4 + z

    places = [(c, y, x, z) for c in range(2) for y in range(4) for x in range(4) for z in range(4)]
    return lax.ppermute(block, ALL, [(index(*p), index(*move(*p))) for p in places])


def swap_u(block, step):
    return permute(block, lambda c, y, x, z: (c, y, x ^ step, z) if c == 0 else (c, y, x, z ^ step))


def swap_y(block, steps):
    return permute(block, lambda c, y, x, z: (c, y ^ steps[c], x, z))


def core():
    return lax.axis_index("peer")


def by_core(first, second):
    return jnp.where(core() == 0, first, second)


def bits(position):
    return (position ^ (position >> 1)) & 1, position >> 1


def parity():
    return (lax.axis_index("tx") + lax.axis_index("tz")) & 1


def tied(*blocks):
    return lax.optimization_barrier(blocks)


def ring(block, axis, prepare=lambda block, step: block):
    far, near, wrap = [
        lax.ppermute(prepare(block, step), axis, [(i, i ^ step) for i in range(4)]) for step in (2, 1, 3)
    ]
    return [block, near, far, wrap]


def turned(block, step, axis):
    size = block.shape[axis] // 4
    parts = [lax.slice_in_dim(block, p * size, (p + 1) * size, axis=axis) for p in range(4)]
    return jnp.concatenate([parts[p ^ FLIP[step]] for p in range(4)], axis=axis)


def gather_logits(block, gain_row, matrix, ints):
    half = block.shape[0] // 2
    tokens = 4 * block.shape[0]
    mine = lax.dynamic_slice_in_dim(block, parity() * half, half, axis=0)
    p = swap_y(mine, (1, 3))
    q = swap_y(mine, (3, 1))
    ints = ring(ints, "dp")
    logits, matrix = add_logits((block,), OWN_PLAN, gain_row, matrix, tokens)
    p, q, logits, *ints = tied(p, q, logits, *ints)
    far = swap_y(q, (1, 3))
    p_side, q_side = swap_u(p, 1), swap_u(q, 3)
    logits, matrix = add_logits((p, q), HELD_PLAN, gain_row, matrix, tokens, logits)
    far, logits = tied(far, logits)
    far_sides = [swap_u(far[: half // 2], 1), swap_u(far[half // 2 :], 3)]
    logits, matrix = add_logits((p_side, q_side, far), OTHER_PLAN, gain_row, matrix, tokens, logits)
    logits, _ = add_logits(far_sides, LAST_PLAN, gain_row, matrix, tokens, logits)
    return logits, [ints[s] for s in (0, 1, 3, 2)]


def make_kernel(count, streamed, loads, stores):
    def kernel(*refs):
        sources = refs[:count]
        gain_ref, head_ref = refs[count : count + 2]
        out_ref, held_head, rows, sums, total, block, sems, head_sems = refs[-8:]
        width = rows.shape[1]
        held = parity() * 64
        p_first = 128 * (NEAR + core() * (WRAP - NEAR))
        q_first = 128 * (NEAR + WRAP) - p_first
        shift = {"all": 0, "held": held, "other": 64 - held}
        shift |= {"p held": p_first + held, "q held": q_first + held}
        shift |= {"p other": p_first + 64 - held, "q other": q_first + 64 - held}
        copies = []
        for source, start, length, target, kind in loads:
            to = pl.multiple_of(shift[kind] + target, 16)
            copies.append(
                pltpu.make_async_copy(
                    sources[source].at[pl.ds(start, length)], rows.at[pl.ds(to, length)], sems.at[len(copies)]
                )
            )
        depth = 1024
        fetches = []
        if streamed:
            for c in range(0, width, depth // 2):
                piece = pl.ds(c, depth // 2)
                fetches.append(
                    pltpu.make_async_copy(head_ref.at[piece], held_head.at[piece], head_sems.at[len(fetches)])
                )
        for copy in copies + fetches:
            copy.start()
        for copy in copies:
            copy.wait()

        @pl.loop(0, rows.shape[0] // 16)
        def _(step):
            piece = pl.ds(pl.multiple_of(step * 16, 16), 16)
            lanes = jnp.zeros((16, TILE), jnp.float32)
            for c in range(0, width, TILE):
                states = rows[piece, c : c + TILE].astype(jnp.float32)
                lanes += states * states
            sums[piece, :] = lanes

        mean = jnp.sum(sums[...], axis=-1, keepdims=True) / width
        sums[...] = jnp.broadcast_to(lax.rsqrt(mean + eps_norm), sums.shape)

        @pl.loop(0, rows.shape[0] // 16)
        def _(step):
            piece = pl.ds(pl.multiple_of(step * 16, 16), 16)
            inverse = sums[piece, :]
            for c in range(0, width, TILE):
                states = rows[piece, c : c + TILE].astype(jnp.float32)
                rows[piece, c : c + TILE] = (states * inverse * gain_ref[:, c : c + TILE]).astype(jnp.bfloat16)

        for c in range(0, width, depth):
            for copy in fetches[2 * c // depth : 2 * c // depth + 2]:
                copy.wait()
            part = jnp.dot(rows[:, c : c + depth], held_head[c : c + depth, :], preferred_element_type=jnp.float32)
            if c == 0:
                total[...] = part
            elif c + depth < width:
                total[...] += part
            else:
                block[...] = (total[...] + part).astype(jnp.bfloat16)
        copies = []
        for start, length, target, kind in stores:
            to = pl.multiple_of(shift[kind] + target, 16)
            copies.append(
                pltpu.make_async_copy(
                    block.at[pl.ds(start, length)], out_ref.at[pl.ds(to, length)], sems.at[len(copies)]
                )
            )
        for copy in copies:
            copy.start()
        for copy in copies:
            copy.wait()

    return kernel


OWN_PLAN = [(0, 0, 128, 0, "all")], [(0, 128, 0, "all")]
HELD_PLAN = [(0, 0, 64, 0, "all"), (1, 0, 64, 64, "all")], [(0, 64, 0, "p held"), (64, 64, 0, "q held")]
OTHER_PLAN = (
    [(0, 0, 64, 0, "all"), (1, 0, 64, 64, "all"), (2, 0, 64, 128, "all")],
    [(0, 64, 0, "p other"), (64, 64, 0, "q other"), (128, 64, FAR * 128, "held")],
)
LAST_PLAN = [(k, 0, 32, 32 * k, "all") for k in range(2)], [(0, 64, FAR * 128, "other")]


def add_logits(sources, plan, gain_row, matrix, tokens, filled=None):
    width, voc = matrix.shape
    anywhere = pl.BlockSpec(memory_space=pl.ANY)
    count = len(sources)
    rows = sum(piece[2] for piece in plan[0])
    streamed = filled is None
    operands = [*sources, gain_row, matrix] + ([] if filled is None else [filled])
    return pl.pallas_call(
        make_kernel(count, streamed, *plan),
        out_shape=(
            jax.ShapeDtypeStruct((tokens, voc), jnp.bfloat16),
            jax.ShapeDtypeStruct(matrix.shape, matrix.dtype),
        ),
        in_specs=[anywhere] * count
        + [pl.BlockSpec(memory_space=pltpu.VMEM), anywhere if streamed else pl.BlockSpec(memory_space=pltpu.VMEM)]
        + ([] if filled is None else [anywhere]),
        out_specs=(anywhere, pl.BlockSpec(memory_space=pltpu.VMEM)),
        scratch_shapes=[
            pltpu.VMEM((rows, width), jnp.bfloat16),
            pltpu.VMEM((rows, TILE), jnp.float32),
            pltpu.VMEM((rows, voc), jnp.float32),
            pltpu.VMEM((rows, voc), jnp.bfloat16),
            pltpu.SemaphoreType.DMA((4,)),
            pltpu.SemaphoreType.DMA((10,)),
        ],
        input_output_aliases={} if streamed else {count + 1: 1, count + 2: 0},
        compiler_params=pltpu.CompilerParams(vmem_limit_bytes=8 * 1024 * 1024),
        cost_estimate=pl.CostEstimate(
            flops=2 * rows * width * voc, bytes_accessed=2 * width * (voc + rows), transcendentals=0
        ),
    )(*operands)


def merge(stats):
    stats = jnp.stack(stats)
    own_max = jnp.max(stats[:, 0], axis=0)
    peer_max = jnp.max(stats[:, 2], axis=0)
    own_scale = jnp.exp(stats[:, 0] - own_max)
    peer_scale = jnp.exp(stats[:, 2] - peer_max)
    (terms,) = tied(
        jnp.stack([stats[:, 1] * own_scale, stats[:, 3] * peer_scale, stats[:, 4], stats[:, 5] * peer_scale])
    )
    own_sum, peer_sum, target, cross = (terms[:, 0] + terms[:, 1]) + (terms[:, 2] + terms[:, 3])
    return jnp.stack([own_max, own_sum, peer_max, peer_sum, target, cross])


def wide(block):
    return block.astype(jnp.float32)


def narrow(block):
    return block.astype(jnp.bfloat16)


def sum_rows(grad_logits, matrix, later):
    voc = grad_logits.shape[1]
    width = matrix.shape[0] // 4
    at_x, at_z = bits(lax.axis_index("tx")), bits(lax.axis_index("tz"))
    rows = grad_logits.reshape(4, 4, 4, 8, voc)
    for axis in (1, 2):
        rows = jnp.concatenate([lax.slice_in_dim(rows, j, j + 1, axis=axis) for j in (0, 3, 1, 2)], axis=axis)
    rows = rows.reshape(4, 2, 2, 2, 2, 8, voc)
    dims = {"xa": (1, at_x[0], "tx", 1), "xb": (2, at_x[1], "tx", 3), "za": (3, at_z[0], "tz", 1), "zb": (4, at_z[1], "tz", 3)}
    orders = [("xa", "xb", "za", "zb"), ("xb", "xa", "zb", "za"), ("za", "zb", "xa", "xb"), ("zb", "za", "xb", "xa")]

    def product(block, q):
        columns = matrix[q * width : (q + 1) * width]
        out = lax.dot_general(
            block.reshape(-1, voc), columns, (((1,), (1,)), ((), ())), preferred_element_type=jnp.float32
        )
        return out.reshape(block.shape[:-1] + (width,))

    def split(block, name):
        at = dims[name][1]
        away = lax.dynamic_index_in_dim(block, 1 - at, 0, keepdims=False)
        return away, lax.dynamic_index_in_dim(block, at, 0, keepdims=False)

    def swap(block, name):
        axis, step = dims[name][2:]
        return lax.ppermute(block, axis, [(i, i ^ step) for i in range(4)])

    sent, stay = [], []
    for q, order in enumerate(orders):
        turned_rows = jnp.transpose(rows, [dims[name][0] for name in order] + [0, 5, 6])
        one, other = split(turned_rows, order[0])
        sent.append(product(*tied(one), q))
        stay.append(split(other, order[1]))
    came = [swap(narrow(sent[q]), orders[q][0]) for q in range(4)]
    came[0], later = tied(came[0], later)
    kept = []
    for q, order in enumerate(orders):
        one, other = [product(part, q) + wide(block) for part, block in zip(stay[q], split(came[q], order[1]))]
        came[q] = swap(narrow(one), order[1])
        kept.append(other)
    for stage in range(2, 4):
        halves = [
            [k + wide(c) for k, c in zip(split(kept[q], orders[q][stage]), split(came[q], orders[q][stage]))]
            for q in range(4)
        ]
        came = [swap(narrow(halves[q][0]), orders[q][stage]) for q in range(4)]
        kept = [halves[q][1] for q in range(4)]
    state = [kept[q] + wide(came[q]) for q in range(4)]
    block = jnp.concatenate(state, axis=-1)
    mine = block[OWN]
    for group, step in ((FAR, 2), (NEAR, 1), (WRAP, 3)):
        mine = mine + wide(swap_y(narrow(block[group]), (step, step)))
    return [mine], later


def shard_stats(logits, peer_logits, hit):
    values = wide(logits)
    own_max = jnp.max(jnp.maximum(values, LOWEST), axis=-1)
    own_sum = jnp.sum(jnp.exp(values - own_max[:, None]), axis=-1)
    target = jnp.sum(jnp.where(hit, values, 0.0), axis=-1)
    own_max, own_sum, target, peer_logits = tied(own_max, own_sum, target, peer_logits)
    peer_values = wide(peer_logits)
    peer_max = jnp.max(jnp.maximum(peer_values, LOWEST), axis=-1)
    peer_exp = jnp.exp(peer_values - peer_max[:, None])
    peer_sum = jnp.sum(peer_exp, axis=-1)
    cross = jnp.sum(peer_exp * (peer_values - values), axis=-1)
    row = lax.broadcasted_iota(jnp.int32, (6, own_max.shape[0]), 0)
    stats = jnp.zeros(row.shape, jnp.float32)
    for k, part in enumerate((own_max, own_sum, peer_max, peer_sum, target, cross)):
        stats = jnp.where(row == k, part[None], stats)
    return stats, peer_logits


def norm_backward_kernel(count, *refs):
    states_ref, gain_ref, out_ref = refs[count:]
    states = states_ref[...]
    width = states.shape[1]
    inverse = lax.rsqrt(jnp.sum(states * states, axis=-1, keepdims=True) / width + eps_norm)
    pieces, start = [], 0
    for ref in refs[:count]:
        columns = slice(start, start + ref.shape[1])
        pieces.append((ref[...] * gain_ref[:, columns], columns))
        start += ref.shape[1]
    inner = sum(jnp.sum(scaled * states[:, columns], axis=-1, keepdims=True) for scaled, columns in pieces) / width
    for scaled, columns in pieces:
        rows = narrow(inverse * (scaled - states[:, columns] * inverse * inverse * inner))
        for k in range(out_ref.shape[0]):
            out_ref[k, :, columns] = rows


def mean_loss(per_token, weights):
    sums = jnp.sum(per_token.reshape(4, -1), axis=-1)
    total = (sums[OWN] + sums[NEAR]) + (sums[FAR] + sums[WRAP])
    return (total / jnp.sum(weights)).reshape((1,))


def local(hidden, gain, head, targets, lengths):
    block = hidden[0]
    gain_row = gain[0][None, :]
    matrix = head[0]
    group = block.shape[0]
    tokens = 4 * group
    voc_shard = matrix.shape[1]
    logits, ints = gather_logits(block, gain_row, matrix, jnp.concatenate([targets, lengths]))
    all_targets = jnp.concatenate([part[:group] for part in ints])
    all_lengths = jnp.concatenate([part[group:] for part in ints])
    peer_logits = lax.ppermute(logits, "peer", [(0, 1), (1, 0)])
    hit = all_targets[:, None] - lax.axis_index(("dp", "tx", "tz")) * voc_shard
    hit = hit == lax.broadcasted_iota(jnp.int32, (1, voc_shard), 1)
    stats, peer_logits = shard_stats(logits, peer_logits, hit)
    stats = merge(ring(stats, "tz"))
    stats = merge(ring(stats, "tx"))
    stats = merge(ring(stats, "dp", lambda block, step: turned(block, step, 1)))
    own_log = stats[0] + jnp.log(stats[1])
    peer_log = stats[2] + jnp.log(stats[3])
    values, peer_values = wide(logits), wide(peer_logits)
    sequence = lax.broadcasted_iota(jnp.int32, (all_lengths.shape[0], tokens), 0)
    token = lax.broadcasted_iota(jnp.int32, sequence.shape, 1)
    limits = jnp.sum(jnp.where(token // LEN == sequence, all_lengths[:, None], 0), axis=0)
    weights = (lax.broadcasted_iota(jnp.int32, (tokens,), 0) % LEN < limits).astype(jnp.float32)

    grad_logits = (
        loss_scale
        * weights[:, None]
        * (
            (1.0 + kl_weight) * jnp.exp(values - own_log[:, None])
            - hit.astype(jnp.float32)
            - kl_weight * jnp.exp(peer_values - peer_log[:, None])
        )
    ).astype(jnp.bfloat16)
    per_token = own_log - stats[4] + kl_weight * (stats[5] / stats[3] - peer_log + own_log)
    grad_normed, per_token = sum_rows(grad_logits, matrix, weights * per_token)
    loss = mean_loss(per_token, weights)

    own = lax.dynamic_slice_in_dim(block, lax.axis_index(("tx", "tz")) * 8, 8, axis=0)
    spread = pl.pallas_call(
        functools.partial(norm_backward_kernel, len(grad_normed)),
        out_shape=jax.ShapeDtypeStruct((16,) + own.shape, own.dtype),
        compiler_params=pltpu.CompilerParams(vmem_limit_bytes=16 * 1024 * 1024),
    )(*grad_normed, wide(own), gain_row)
    grad_hidden = lax.all_to_all(spread, ("tx", "tz"), split_axis=0, concat_axis=0, tiled=True)
    return (loss, grad_hidden.reshape((1,) + block.shape))


def solution(mesh):
    cube = Mesh(mesh.devices.reshape(2, 4, 4, 4), ALL)
    return jax.shard_map(
        local,
        mesh=cube,
        in_specs=(
            P("peer", "dp", None),
            P("peer", None),
            P("peer", None, ("dp", "tx", "tz")),
            P("dp"),
            P("dp"),
        ),
        out_specs=(P("peer"), P("peer", "dp", None)),
        check_vma=False,
    )
```

```python
import functools

import jax
import jax.numpy as jnp
from jax import lax
from jax.experimental import pallas as pl
from jax.experimental.pallas import tpu as pltpu
from jax.sharding import Mesh, PartitionSpec as P

LEN = 32
TILE = 128

kl_weight = 0.5
loss_scale = 64.0
eps_norm = 1e-06

LOWEST = -3.4e38

ALL = ("peer", "dp", "tx", "tz")

OWN, NEAR, WRAP, FAR = range(4)
FLIP = {1: 1, 2: 3, 3: 2}


def permute(block, move):
    def index(core, y, x, z):
        return ((core * 4 + y) * 4 + x) * 4 + z

    places = [(c, y, x, z) for c in range(2) for y in range(4) for x in range(4) for z in range(4)]
    return lax.ppermute(block, ALL, [(index(*p), index(*move(*p))) for p in places])


def swap_u(block, step):
    return permute(block, lambda c, y, x, z: (c, y, x ^ step, z) if c == 0 else (c, y, x, z ^ step))


def swap_y(block, steps):
    return permute(block, lambda c, y, x, z: (c, y ^ steps[c], x, z))


def core():
    return lax.axis_index("peer")


def by_core(first, second):
    return jnp.where(core() == 0, first, second)


def bits(position):
    return (position ^ (position >> 1)) & 1, position >> 1


def parity():
    return (lax.axis_index("tx") + lax.axis_index("tz")) & 1


def tied(*blocks):
    return lax.optimization_barrier(blocks)


def ring(block, axis, prepare=lambda block, step: block):
    far, near, wrap = [
        lax.ppermute(prepare(block, step), axis, [(i, i ^ step) for i in range(4)]) for step in (2, 1, 3)
    ]
    return [block, near, far, wrap]


def turned(block, step, axis):
    size = block.shape[axis] // 4
    parts = [lax.slice_in_dim(block, p * size, (p + 1) * size, axis=axis) for p in range(4)]
    return jnp.concatenate([parts[p ^ FLIP[step]] for p in range(4)], axis=axis)


def gather_logits(block, gain_row, matrix, ints):
    half = block.shape[0] // 2
    tokens = 4 * block.shape[0]
    mine = lax.dynamic_slice_in_dim(block, parity() * half, half, axis=0)
    p = swap_y(mine, (1, 3))
    q = swap_y(mine, (3, 1))
    ints = ring(ints, "dp")
    logits, matrix = add_logits((block,), OWN_PLAN, gain_row, matrix, tokens)
    p, q, logits, *ints = tied(p, q, logits, *ints)
    far = swap_y(q, (1, 3))
    p_side, q_side = swap_u(p, 1), swap_u(q, 3)
    logits, matrix = add_logits((p, q), HELD_PLAN, gain_row, matrix, tokens, logits)
    far, logits = tied(far, logits)
    far_sides = [swap_u(far[: half // 2], 1), swap_u(far[half // 2 :], 3)]
    logits, matrix = add_logits((p_side, q_side), OTHER_PLAN, gain_row, matrix, tokens, logits)
    logits, _ = add_logits((far, *far_sides), FAR_PLAN, gain_row, matrix, tokens, logits)
    return logits, [ints[s] for s in (0, 1, 3, 2)]


def make_kernel(count, streamed, loads, stores):
    def kernel(*refs):
        sources = refs[:count]
        gain_ref, head_ref = refs[count : count + 2]
        out_ref, held_head, rows, sums, total, block, sems, head_sems = refs[-8:]
        width = rows.shape[1]
        held = parity() * 64
        p_first = 128 * (NEAR + core() * (WRAP - NEAR))
        q_first = 128 * (NEAR + WRAP) - p_first
        shift = {"all": 0, "held": held, "other": 64 - held}
        shift |= {"p held": p_first + held, "q held": q_first + held}
        shift |= {"p other": p_first + 64 - held, "q other": q_first + 64 - held}
        copies = []
        for source, start, length, target, kind in loads:
            to = pl.multiple_of(shift[kind] + target, 16)
            copies.append(
                pltpu.make_async_copy(
                    sources[source].at[pl.ds(start, length)], rows.at[pl.ds(to, length)], sems.at[len(copies)]
                )
            )
        depth = 1024
        fetches = []
        if streamed:
            for c in range(0, width, depth // 2):
                piece = pl.ds(c, depth // 2)
                fetches.append(
                    pltpu.make_async_copy(head_ref.at[piece], held_head.at[piece], head_sems.at[len(fetches)])
                )
        for copy in copies + fetches:
            copy.start()
        for copy in copies:
            copy.wait()

        @pl.loop(0, rows.shape[0] // 16)
        def _(step):
            piece = pl.ds(pl.multiple_of(step * 16, 16), 16)
            lanes = jnp.zeros((16, TILE), jnp.float32)
            for c in range(0, width, TILE):
                states = rows[piece, c : c + TILE].astype(jnp.float32)
                lanes += states * states
            sums[piece, :] = lanes

        mean = jnp.sum(sums[...], axis=-1, keepdims=True) / width
        sums[...] = jnp.broadcast_to(lax.rsqrt(mean + eps_norm), sums.shape)

        @pl.loop(0, rows.shape[0] // 16)
        def _(step):
            piece = pl.ds(pl.multiple_of(step * 16, 16), 16)
            inverse = sums[piece, :]
            for c in range(0, width, TILE):
                states = rows[piece, c : c + TILE].astype(jnp.float32)
                rows[piece, c : c + TILE] = (states * inverse * gain_ref[:, c : c + TILE]).astype(jnp.bfloat16)

        for c in range(0, width, depth):
            for copy in fetches[2 * c // depth : 2 * c // depth + 2]:
                copy.wait()
            part = jnp.dot(rows[:, c : c + depth], held_head[c : c + depth, :], preferred_element_type=jnp.float32)
            if c == 0:
                total[...] = part
            elif c + depth < width:
                total[...] += part
            else:
                block[...] = (total[...] + part).astype(jnp.bfloat16)
        copies = []
        for start, length, target, kind in stores:
            to = pl.multiple_of(shift[kind] + target, 16)
            copies.append(
                pltpu.make_async_copy(
                    block.at[pl.ds(start, length)], out_ref.at[pl.ds(to, length)], sems.at[len(copies)]
                )
            )
        for copy in copies:
            copy.start()
        for copy in copies:
            copy.wait()

    return kernel


OWN_PLAN = [(0, 0, 128, 0, "all")], [(0, 128, 0, "all")]
HELD_PLAN = [(0, 0, 64, 0, "all"), (1, 0, 64, 64, "all")], [(0, 64, 0, "p held"), (64, 64, 0, "q held")]
OTHER_PLAN = [(0, 0, 64, 0, "all"), (1, 0, 64, 64, "all")], [(0, 64, 0, "p other"), (64, 64, 0, "q other")]
FAR_PLAN = (
    [(0, 0, 64, 0, "held")] + [(1 + k, 0, 32, 32 * k, "other") for k in range(2)],
    [(0, 128, FAR * 128, "all")],
)


def add_logits(sources, plan, gain_row, matrix, tokens, filled=None):
    width, voc = matrix.shape
    anywhere = pl.BlockSpec(memory_space=pl.ANY)
    count = len(sources)
    rows = sum(piece[2] for piece in plan[0])
    streamed = filled is None
    operands = [*sources, gain_row, matrix] + ([] if filled is None else [filled])
    return pl.pallas_call(
        make_kernel(count, streamed, *plan),
        out_shape=(
            jax.ShapeDtypeStruct((tokens, voc), jnp.bfloat16),
            jax.ShapeDtypeStruct(matrix.shape, matrix.dtype),
        ),
        in_specs=[anywhere] * count
        + [pl.BlockSpec(memory_space=pltpu.VMEM), anywhere if streamed else pl.BlockSpec(memory_space=pltpu.VMEM)]
        + ([] if filled is None else [anywhere]),
        out_specs=(anywhere, pl.BlockSpec(memory_space=pltpu.VMEM)),
        scratch_shapes=[
            pltpu.VMEM((rows, width), jnp.bfloat16),
            pltpu.VMEM((rows, TILE), jnp.float32),
            pltpu.VMEM((rows, voc), jnp.float32),
            pltpu.VMEM((rows, voc), jnp.bfloat16),
            pltpu.SemaphoreType.DMA((4,)),
            pltpu.SemaphoreType.DMA((10,)),
        ],
        input_output_aliases={} if streamed else {count + 1: 1, count + 2: 0},
        compiler_params=pltpu.CompilerParams(vmem_limit_bytes=8 * 1024 * 1024),
        cost_estimate=pl.CostEstimate(
            flops=2 * rows * width * voc, bytes_accessed=2 * width * (voc + rows), transcendentals=0
        ),
    )(*operands)


def merge(stats):
    stats = jnp.stack(stats)
    own_max = jnp.max(stats[:, 0], axis=0)
    peer_max = jnp.max(stats[:, 2], axis=0)
    own_scale = jnp.exp(stats[:, 0] - own_max)
    peer_scale = jnp.exp(stats[:, 2] - peer_max)
    (terms,) = tied(
        jnp.stack([stats[:, 1] * own_scale, stats[:, 3] * peer_scale, stats[:, 4], stats[:, 5] * peer_scale])
    )
    own_sum, peer_sum, target, cross = (terms[:, 0] + terms[:, 1]) + (terms[:, 2] + terms[:, 3])
    return jnp.stack([own_max, own_sum, peer_max, peer_sum, target, cross])


def wide(block):
    return block.astype(jnp.float32)


def narrow(block):
    return block.astype(jnp.bfloat16)


def sum_rows(grad_logits, matrix, later):
    voc = grad_logits.shape[1]
    width = matrix.shape[0] // 4
    at_x, at_z = bits(lax.axis_index("tx")), bits(lax.axis_index("tz"))
    rows = grad_logits.reshape(4, 4, 4, 8, voc)
    for axis in (1, 2):
        rows = jnp.concatenate([lax.slice_in_dim(rows, j, j + 1, axis=axis) for j in (0, 3, 1, 2)], axis=axis)
    rows = rows.reshape(4, 2, 2, 2, 2, 8, voc)
    dims = {"xa": (1, at_x[0], "tx", 1), "xb": (2, at_x[1], "tx", 3), "za": (3, at_z[0], "tz", 1), "zb": (4, at_z[1], "tz", 3)}
    orders = [("xa", "xb", "za", "zb"), ("xb", "xa", "zb", "za"), ("za", "zb", "xa", "xb"), ("zb", "za", "xb", "xa")]

    def product(block, q):
        columns = matrix[q * width : (q + 1) * width]
        out = lax.dot_general(
            block.reshape(-1, voc), columns, (((1,), (1,)), ((), ())), preferred_element_type=jnp.float32
        )
        return out.reshape(block.shape[:-1] + (width,))

    def split(block, name):
        at = dims[name][1]
        away = lax.dynamic_index_in_dim(block, 1 - at, 0, keepdims=False)
        return away, lax.dynamic_index_in_dim(block, at, 0, keepdims=False)

    def swap(block, name):
        axis, step = dims[name][2:]
        return lax.ppermute(block, axis, [(i, i ^ step) for i in range(4)])

    sent, stay = [], []
    for q, order in enumerate(orders):
        turned_rows = jnp.transpose(rows, [dims[name][0] for name in order] + [0, 5, 6])
        one, other = split(turned_rows, order[0])
        sent.append(product(*tied(one), q))
        stay.append(split(other, order[1]))
    came = [swap(narrow(sent[q]), orders[q][0]) for q in range(4)]
    came[0], later = tied(came[0], later)
    kept = []
    for q, order in enumerate(orders):
        one, other = [product(part, q) + wide(block) for part, block in zip(stay[q], split(came[q], order[1]))]
        came[q] = swap(narrow(one), order[1])
        kept.append(other)
    for stage in range(2, 4):
        halves = [
            [k + wide(c) for k, c in zip(split(kept[q], orders[q][stage]), split(came[q], orders[q][stage]))]
            for q in range(4)
        ]
        came = [swap(narrow(halves[q][0]), orders[q][stage]) for q in range(4)]
        kept = [halves[q][1] for q in range(4)]
    state = [kept[q] + wide(came[q]) for q in range(4)]
    block = jnp.concatenate(state, axis=-1)
    mine = block[OWN]
    for group, step in ((FAR, 2), (NEAR, 1), (WRAP, 3)):
        mine = mine + wide(swap_y(narrow(block[group]), (step, step)))
    return [mine], later


def shard_stats(logits, peer_logits, hit):
    values = wide(logits)
    own_max = jnp.max(jnp.maximum(values, LOWEST), axis=-1)
    own_sum = jnp.sum(jnp.exp(values - own_max[:, None]), axis=-1)
    target = jnp.sum(jnp.where(hit, values, 0.0), axis=-1)
    own_max, own_sum, target, peer_logits = tied(own_max, own_sum, target, peer_logits)
    peer_values = wide(peer_logits)
    peer_max = jnp.max(jnp.maximum(peer_values, LOWEST), axis=-1)
    peer_exp = jnp.exp(peer_values - peer_max[:, None])
    peer_sum = jnp.sum(peer_exp, axis=-1)
    cross = jnp.sum(peer_exp * (peer_values - values), axis=-1)
    row = lax.broadcasted_iota(jnp.int32, (6, own_max.shape[0]), 0)
    stats = jnp.zeros(row.shape, jnp.float32)
    for k, part in enumerate((own_max, own_sum, peer_max, peer_sum, target, cross)):
        stats = jnp.where(row == k, part[None], stats)
    return stats, peer_logits


def norm_backward_kernel(count, *refs):
    states_ref, gain_ref, out_ref = refs[count:]
    states = states_ref[...]
    width = states.shape[1]
    inverse = lax.rsqrt(jnp.sum(states * states, axis=-1, keepdims=True) / width + eps_norm)
    pieces, start = [], 0
    for ref in refs[:count]:
        columns = slice(start, start + ref.shape[1])
        pieces.append((ref[...] * gain_ref[:, columns], columns))
        start += ref.shape[1]
    inner = sum(jnp.sum(scaled * states[:, columns], axis=-1, keepdims=True) for scaled, columns in pieces) / width
    for scaled, columns in pieces:
        rows = narrow(inverse * (scaled - states[:, columns] * inverse * inverse * inner))
        for k in range(out_ref.shape[0]):
            out_ref[k, :, columns] = rows


def mean_loss(per_token, weights):
    sums = jnp.sum(per_token.reshape(4, -1), axis=-1)
    total = (sums[OWN] + sums[NEAR]) + (sums[FAR] + sums[WRAP])
    return (total / jnp.sum(weights)).reshape((1,))


def local(hidden, gain, head, targets, lengths):
    block = hidden[0]
    gain_row = gain[0][None, :]
    matrix = head[0]
    group = block.shape[0]
    tokens = 4 * group
    voc_shard = matrix.shape[1]
    logits, ints = gather_logits(block, gain_row, matrix, jnp.concatenate([targets, lengths]))
    all_targets = jnp.concatenate([part[:group] for part in ints])
    all_lengths = jnp.concatenate([part[group:] for part in ints])
    peer_logits = lax.ppermute(logits, "peer", [(0, 1), (1, 0)])
    hit = all_targets[:, None] - lax.axis_index(("dp", "tx", "tz")) * voc_shard
    hit = hit == lax.broadcasted_iota(jnp.int32, (1, voc_shard), 1)
    stats, peer_logits = shard_stats(logits, peer_logits, hit)
    stats = merge(ring(stats, "tz"))
    stats = merge(ring(stats, "tx"))
    stats = merge(ring(stats, "dp", lambda block, step: turned(block, step, 1)))
    own_log = stats[0] + jnp.log(stats[1])
    peer_log = stats[2] + jnp.log(stats[3])
    values, peer_values = wide(logits), wide(peer_logits)
    sequence = lax.broadcasted_iota(jnp.int32, (all_lengths.shape[0], tokens), 0)
    token = lax.broadcasted_iota(jnp.int32, sequence.shape, 1)
    limits = jnp.sum(jnp.where(token // LEN == sequence, all_lengths[:, None], 0), axis=0)
    weights = (lax.broadcasted_iota(jnp.int32, (tokens,), 0) % LEN < limits).astype(jnp.float32)

    grad_logits = (
        loss_scale
        * weights[:, None]
        * (
            (1.0 + kl_weight) * jnp.exp(values - own_log[:, None])
            - hit.astype(jnp.float32)
            - kl_weight * jnp.exp(peer_values - peer_log[:, None])
        )
    ).astype(jnp.bfloat16)
    per_token = own_log - stats[4] + kl_weight * (stats[5] / stats[3] - peer_log + own_log)
    grad_normed, per_token = sum_rows(grad_logits, matrix, weights * per_token)
    loss = mean_loss(per_token, weights)

    own = lax.dynamic_slice_in_dim(block, lax.axis_index(("tx", "tz")) * 8, 8, axis=0)
    spread = pl.pallas_call(
        functools.partial(norm_backward_kernel, len(grad_normed)),
        out_shape=jax.ShapeDtypeStruct((16,) + own.shape, own.dtype),
        compiler_params=pltpu.CompilerParams(vmem_limit_bytes=16 * 1024 * 1024),
    )(*grad_normed, wide(own), gain_row)
    grad_hidden = lax.all_to_all(spread, ("tx", "tz"), split_axis=0, concat_axis=0, tiled=True)
    return (loss, grad_hidden.reshape((1,) + block.shape))


def solution(mesh):
    cube = Mesh(mesh.devices.reshape(2, 4, 4, 4), ALL)
    return jax.shard_map(
        local,
        mesh=cube,
        in_specs=(
            P("peer", "dp", None),
            P("peer", None),
            P("peer", None, ("dp", "tx", "tz")),
            P("dp"),
            P("dp"),
        ),
        out_specs=(P("peer"), P("peer", "dp", None)),
        check_vma=False,
    )
```

```python
import functools

import jax
import jax.numpy as jnp
from jax import lax
from jax.experimental import pallas as pl
from jax.experimental.pallas import tpu as pltpu
from jax.sharding import Mesh, PartitionSpec as P

LEN = 32
TILE = 128

kl_weight = 0.5
loss_scale = 64.0
eps_norm = 1e-06

ALL = ("peer", "dp", "tx", "tz")

OWN, NEAR, WRAP, FAR = range(4)
FLIP = {1: 1, 2: 3, 3: 2}


def permute(block, move):
    def index(core, y, x, z):
        return ((core * 4 + y) * 4 + x) * 4 + z

    places = [(c, y, x, z) for c in range(2) for y in range(4) for x in range(4) for z in range(4)]
    return lax.ppermute(block, ALL, [(index(*p), index(*move(*p))) for p in places])


def swap_u(block, step):
    return permute(block, lambda c, y, x, z: (c, y, x ^ step, z) if c == 0 else (c, y, x, z ^ step))


def swap_y(block, steps):
    return permute(block, lambda c, y, x, z: (c, y ^ steps[c], x, z))


def core():
    return lax.axis_index("peer")


def by_core(first, second):
    return jnp.where(core() == 0, first, second)


def bits(position):
    return (position ^ (position >> 1)) & 1, position >> 1


def parity():
    return (lax.axis_index("tx") + lax.axis_index("tz")) & 1


def tied(*blocks):
    return lax.optimization_barrier(blocks)


def ring(block, axis):
    far, near, wrap = [lax.ppermute(block, axis, [(i, i ^ s) for i in range(4)]) for s in (2, 1, 3)]
    return [block, near, far, wrap]


def turned(block, step, axis):
    size = block.shape[axis] // 4
    parts = [lax.slice_in_dim(block, p * size, (p + 1) * size, axis=axis) for p in range(4)]
    return jnp.concatenate([parts[p ^ FLIP[step]] for p in range(4)], axis=axis)


def gather_logits(block, gain_row, matrix, ints):
    half = block.shape[0] // 2
    tokens = 4 * block.shape[0]
    mine = lax.dynamic_slice_in_dim(block, parity() * half, half, axis=0)
    p = swap_y(mine, (1, 3))
    q = swap_y(mine, (3, 1))
    ints = ring(ints, "dp")
    logits = add_logits((block,), OWN_PLAN, gain_row, matrix, tokens)
    p, q, logits, *ints = tied(p, q, logits, *ints)
    far = swap_y(q, (1, 3))
    p_side, q_side = swap_u(p, 1), swap_u(q, 3)
    logits = add_logits((p, q), HELD_PLAN, gain_row, matrix, tokens, logits)
    far, logits = tied(far, logits)
    far_sides = [swap_u(far[: half // 2], 1), swap_u(far[half // 2 :], 3)]
    logits = add_logits((p_side, q_side), OTHER_PLAN, gain_row, matrix, tokens, logits)
    logits = add_logits((far, *far_sides), FAR_PLAN, gain_row, matrix, tokens, logits)
    return logits, [ints[s] for s in (0, 1, 3, 2)]


def make_kernel(count, loads, stores):
    def kernel(*refs):
        sources = refs[:count]
        gain_ref, head_ref = refs[count : count + 2]
        out_ref, rows, sums, total, block, sems = refs[-6:]
        width = rows.shape[1]
        held = parity() * 64
        p_first = 128 * (NEAR + core() * (WRAP - NEAR))
        q_first = 128 * (NEAR + WRAP) - p_first
        shift = {"all": 0, "held": held, "other": 64 - held}
        shift |= {"p held": p_first + held, "q held": q_first + held}
        shift |= {"p other": p_first + 64 - held, "q other": q_first + 64 - held}
        copies = []
        for source, start, length, target, kind in loads:
            to = pl.multiple_of(shift[kind] + target, 16)
            copies.append(
                pltpu.make_async_copy(
                    sources[source].at[pl.ds(start, length)], rows.at[pl.ds(to, length)], sems.at[len(copies)]
                )
            )
        for copy in copies:
            copy.start()
        for copy in copies:
            copy.wait()

        @pl.loop(0, rows.shape[0] // 16)
        def _(step):
            piece = pl.ds(pl.multiple_of(step * 16, 16), 16)
            lanes = jnp.zeros((16, TILE), jnp.float32)
            for c in range(0, width, TILE):
                states = rows[piece, c : c + TILE].astype(jnp.float32)
                lanes += states * states
            sums[piece, :] = lanes

        mean = jnp.sum(sums[...], axis=-1, keepdims=True) / width
        sums[...] = jnp.broadcast_to(lax.rsqrt(mean + eps_norm), sums.shape)

        @pl.loop(0, rows.shape[0] // 16)
        def _(step):
            piece = pl.ds(pl.multiple_of(step * 16, 16), 16)
            inverse = sums[piece, :]
            for c in range(0, width, TILE):
                states = rows[piece, c : c + TILE].astype(jnp.float32)
                rows[piece, c : c + TILE] = (states * inverse * gain_ref[:, c : c + TILE]).astype(jnp.bfloat16)

        depth = 1024
        for c in range(0, width, depth):
            part = jnp.dot(rows[:, c : c + depth], head_ref[c : c + depth, :], preferred_element_type=jnp.float32)
            if c == 0:
                total[...] = part
            elif c + depth < width:
                total[...] += part
            else:
                block[...] = (total[...] + part).astype(jnp.bfloat16)
        copies = []
        for start, length, target, kind in stores:
            to = pl.multiple_of(shift[kind] + target, 16)
            copies.append(
                pltpu.make_async_copy(
                    block.at[pl.ds(start, length)], out_ref.at[pl.ds(to, length)], sems.at[len(copies)]
                )
            )
        for copy in copies:
            copy.start()
        for copy in copies:
            copy.wait()

    return kernel


OWN_PLAN = [(0, 0, 128, 0, "all")], [(0, 128, 0, "all")]
HELD_PLAN = [(0, 0, 64, 0, "all"), (1, 0, 64, 64, "all")], [(0, 64, 0, "p held"), (64, 64, 0, "q held")]
OTHER_PLAN = [(0, 0, 64, 0, "all"), (1, 0, 64, 64, "all")], [(0, 64, 0, "p other"), (64, 64, 0, "q other")]
FAR_PLAN = (
    [(0, 0, 64, 0, "held")] + [(1 + k, 0, 32, 32 * k, "other") for k in range(2)],
    [(0, 128, FAR * 128, "all")],
)


def add_logits(sources, plan, gain_row, matrix, tokens, filled=None):
    width, voc = matrix.shape
    anywhere = pl.BlockSpec(memory_space=pl.ANY)
    count = len(sources)
    rows = sum(piece[2] for piece in plan[0])
    operands = [*sources, gain_row, matrix] + ([] if filled is None else [filled])
    return pl.pallas_call(
        make_kernel(count, *plan),
        out_shape=jax.ShapeDtypeStruct((tokens, voc), jnp.bfloat16),
        in_specs=[anywhere] * count
        + [pl.BlockSpec(memory_space=pltpu.VMEM)] * 2
        + ([] if filled is None else [anywhere]),
        out_specs=anywhere,
        scratch_shapes=[
            pltpu.VMEM((rows, width), jnp.bfloat16),
            pltpu.VMEM((rows, TILE), jnp.float32),
            pltpu.VMEM((rows, voc), jnp.float32),
            pltpu.VMEM((rows, voc), jnp.bfloat16),
            pltpu.SemaphoreType.DMA((4,)),
        ],
        input_output_aliases={} if filled is None else {count + 2: 0},
        compiler_params=pltpu.CompilerParams(vmem_limit_bytes=8 * 1024 * 1024),
        cost_estimate=pl.CostEstimate(
            flops=2 * rows * width * voc, bytes_accessed=2 * width * (voc + rows), transcendentals=0
        ),
    )(*operands)


def merge(stats):
    stats = jnp.stack(stats)
    own_max = jnp.max(stats[:, 0], axis=0)
    peer_max = jnp.max(stats[:, 2], axis=0)
    own_scale = jnp.exp(stats[:, 0] - own_max)
    peer_scale = jnp.exp(stats[:, 2] - peer_max)
    (terms,) = tied(
        jnp.stack([stats[:, 1] * own_scale, stats[:, 3] * peer_scale, stats[:, 4], stats[:, 5] * peer_scale])
    )
    own_sum, peer_sum, target, cross = (terms[:, 0] + terms[:, 1]) + (terms[:, 2] + terms[:, 3])
    return jnp.stack([own_max, own_sum, peer_max, peer_sum, target, cross])


def wide(block):
    return block.astype(jnp.float32)


def narrow(block):
    return block.astype(jnp.bfloat16)


def sum_rows(grad_logits, matrix, later):
    voc = grad_logits.shape[1]
    width = matrix.shape[0] // 4
    at_x, at_z = bits(lax.axis_index("tx")), bits(lax.axis_index("tz"))
    rows = grad_logits.reshape(4, 4, 4, 8, voc)
    for axis in (1, 2):
        rows = jnp.concatenate([lax.slice_in_dim(rows, j, j + 1, axis=axis) for j in (0, 3, 1, 2)], axis=axis)
    rows = rows.reshape(4, 2, 2, 2, 2, 8, voc)
    dims = {"xa": (1, at_x[0], "tx", 1), "xb": (2, at_x[1], "tx", 3), "za": (3, at_z[0], "tz", 1), "zb": (4, at_z[1], "tz", 3)}
    orders = [("xa", "xb", "za", "zb"), ("xb", "xa", "zb", "za"), ("za", "zb", "xa", "xb"), ("zb", "za", "xb", "xa")]

    def product(block, q):
        columns = matrix[q * width : (q + 1) * width]
        out = lax.dot_general(
            block.reshape(-1, voc), columns, (((1,), (1,)), ((), ())), preferred_element_type=jnp.float32
        )
        return out.reshape(block.shape[:-1] + (width,))

    def split(block, name):
        at = dims[name][1]
        away = lax.dynamic_index_in_dim(block, 1 - at, 0, keepdims=False)
        return away, lax.dynamic_index_in_dim(block, at, 0, keepdims=False)

    def swap(block, name):
        axis, step = dims[name][2:]
        return lax.ppermute(block, axis, [(i, i ^ step) for i in range(4)])

    sent, stay = [], []
    for q, order in enumerate(orders):
        turned_rows = jnp.transpose(rows, [dims[name][0] for name in order] + [0, 5, 6])
        one, other = split(turned_rows, order[0])
        sent.append(product(*tied(one), q))
        stay.append(split(other, order[1]))
    came = [swap(narrow(sent[q]), orders[q][0]) for q in range(4)]
    came[0], later = tied(came[0], later)
    kept = []
    for q, order in enumerate(orders):
        one, other = [product(part, q) + wide(block) for part, block in zip(stay[q], split(came[q], order[1]))]
        came[q] = swap(narrow(one), order[1])
        kept.append(other)
    for stage in range(2, 4):
        halves = [
            [k + wide(c) for k, c in zip(split(kept[q], orders[q][stage]), split(came[q], orders[q][stage]))]
            for q in range(4)
        ]
        came = [swap(narrow(halves[q][0]), orders[q][stage]) for q in range(4)]
        kept = [halves[q][1] for q in range(4)]
    state = [kept[q] + wide(came[q]) for q in range(4)]
    block = jnp.concatenate(state, axis=-1)
    mine = block[OWN]
    for group, step in ((FAR, 2), (NEAR, 1), (WRAP, 3)):
        mine = mine + wide(swap_y(narrow(block[group]), (step, step)))
    return [mine], later


def shard_stats(logits, peer_logits, hit):
    values = wide(logits)
    own_max = jnp.max(values, axis=-1)
    own_sum = jnp.sum(jnp.exp(values - own_max[:, None]), axis=-1)
    target = jnp.sum(jnp.where(hit, values, 0.0), axis=-1)
    own_max, own_sum, target, peer_logits = tied(own_max, own_sum, target, peer_logits)
    peer_values = wide(peer_logits)
    peer_max = jnp.max(peer_values, axis=-1)
    peer_exp = jnp.exp(peer_values - peer_max[:, None])
    peer_sum = jnp.sum(peer_exp, axis=-1)
    cross = jnp.sum(peer_exp * (peer_values - values), axis=-1)
    return jnp.stack([own_max, own_sum, peer_max, peer_sum, target, cross]), peer_logits


def norm_backward_kernel(count, *refs):
    states_ref, gain_ref, out_ref = refs[count:]
    states = states_ref[...]
    width = states.shape[1]
    inverse = lax.rsqrt(jnp.sum(states * states, axis=-1, keepdims=True) / width + eps_norm)
    pieces, start = [], 0
    for ref in refs[:count]:
        columns = slice(start, start + ref.shape[1])
        pieces.append((ref[...] * gain_ref[:, columns], columns))
        start += ref.shape[1]
    inner = sum(jnp.sum(scaled * states[:, columns], axis=-1, keepdims=True) for scaled, columns in pieces) / width
    for scaled, columns in pieces:
        rows = narrow(inverse * (scaled - states[:, columns] * inverse * inverse * inner))
        for k in range(out_ref.shape[0]):
            out_ref[k, :, columns] = rows


def mean_loss(stats, weights):
    own_log = stats[0] + jnp.log(stats[1])
    peer_log = stats[2] + jnp.log(stats[3])
    per_token = own_log - stats[4] + kl_weight * (stats[5] / stats[3] - peer_log + own_log)
    sums = jnp.sum((weights * per_token).reshape(4, -1), axis=-1)
    total = (sums[OWN] + sums[NEAR]) + (sums[FAR] + sums[WRAP])
    return (total / jnp.sum(weights)).reshape((1,))


def local(hidden, gain, head, targets, lengths):
    block = hidden[0]
    gain_row = gain[0][None, :]
    matrix = head[0]
    group = block.shape[0]
    tokens = 4 * group
    voc_shard = matrix.shape[1]
    logits, ints = gather_logits(block, gain_row, matrix, jnp.concatenate([targets, lengths]))
    all_targets = jnp.concatenate([part[:group] for part in ints])
    all_lengths = jnp.concatenate([part[group:] for part in ints])
    peer_logits = lax.ppermute(logits, "peer", [(0, 1), (1, 0)])
    hit = all_targets[:, None] - lax.axis_index(("dp", "tx", "tz")) * voc_shard
    hit = hit == lax.broadcasted_iota(jnp.int32, (1, voc_shard), 1)
    stats, peer_logits = shard_stats(logits, peer_logits, hit)
    stats = merge(ring(stats, "tz"))
    stats = merge(ring(stats, "tx"))
    stats = ring(stats, "dp")
    stats = merge([stats[0]] + [turned(stats[s], s, 1) for s in (1, 2, 3)])
    own_log = stats[0] + jnp.log(stats[1])
    peer_log = stats[2] + jnp.log(stats[3])
    values, peer_values = wide(logits), wide(peer_logits)
    position = lax.broadcasted_iota(jnp.int32, (tokens // LEN, LEN), 1)
    weights = (position < all_lengths[:, None]).astype(jnp.float32).reshape(tokens)

    grad_logits = (
        loss_scale
        * weights[:, None]
        * (
            (1.0 + kl_weight) * jnp.exp(values - own_log[:, None])
            - hit.astype(jnp.float32)
            - kl_weight * jnp.exp(peer_values - peer_log[:, None])
        )
    ).astype(jnp.bfloat16)
    grad_normed, stats = sum_rows(grad_logits, matrix, stats)
    loss = mean_loss(stats, weights)

    own = lax.dynamic_slice_in_dim(block, lax.axis_index(("tx", "tz")) * 8, 8, axis=0)
    spread = pl.pallas_call(
        functools.partial(norm_backward_kernel, len(grad_normed)),
        out_shape=jax.ShapeDtypeStruct((16,) + own.shape, own.dtype),
        compiler_params=pltpu.CompilerParams(vmem_limit_bytes=16 * 1024 * 1024),
    )(*grad_normed, wide(own), gain_row)
    grad_hidden = lax.all_to_all(spread, ("tx", "tz"), split_axis=0, concat_axis=0, tiled=True)
    return (loss, grad_hidden.reshape((1,) + block.shape))


def solution(mesh):
    cube = Mesh(mesh.devices.reshape(2, 4, 4, 4), ALL)
    return jax.shard_map(
        local,
        mesh=cube,
        in_specs=(
            P("peer", "dp", None),
            P("peer", None),
            P("peer", None, ("dp", "tx", "tz")),
            P("dp"),
            P("dp"),
        ),
        out_specs=(P("peer"), P("peer", "dp", None)),
        check_vma=False,
    )
```
